256 devices in a mesh: section: 4 (over x), seq: 16 (over y, z_hi, core), mp: 4 (over z_lo).
Axes of the slice: x: 4, y: 4, z: 8 (z_hi: 2, z_lo: 4; z = z_hi * 4 + z_lo), core: 2. Of those that a mesh axis runs over, the one named last changes fastest.
Arguments:
- rows40: bfloat16 [3072, 8192], P('seq', ('section', 'mp')), may hold values from -6 to 6
- queries: bfloat16 [4, 3072, 4096], P('section', 'seq', 'mp'), may hold values from -200 to 200, as said below
- kv_weight: bfloat16 [4, 8192, 1024], P('section', 'seq', 'mp'), may hold values from -0.0625 to 0.0625
- out_grad: bfloat16 [4, 3072, 4096], P('section', 'seq', 'mp'), may hold values from -6 to 6
- block_order: int32 [64], replicated, may hold values from 0 to 63, each once
Outputs:
- attended: bfloat16 [4, 3072, 4096], P('section', 'seq', 'mp')
- query_grad: bfloat16 [4, 3072, 4096], P('section', 'seq', 'mp')
- kv_weight_grad: float32 [4, 8192, 1024], P('section', 'seq', 'mp')
The draws below stay inside these ranges and needn't reach their ends.
Inputs may be any that keep to these rules, and one draw needn't show every extreme that they name: `queries`: rows drawn about normal; a layer's rows may differ in scale. `block_order`: A permutation of the position blocks.
All inputs are finite; a program needn't handle non-finite values.
Results may differ from the reference program's by a relative error of at most 0.035.
The reference program's roundings to bfloat16 on the way count: a program that leaves them out, or rounds other values in their place, can miss the bound.
Values may be sent and summed in bfloat16 or wider, within the bound.
A program may use at most 64 MiB of HBM per device.

```python
from functools import partial
import jax
import jax.numpy as jnp
from jax import lax

D = 8192
HEADS = 32
KV_HEADS = 4
HD = 128
SLOTS = 4
TOK_DEV = 192
TOKENS = 3072
LAYERS = 4
N_SEQ = 16


def draw_queries(key, part):
    key = jax.random.fold_in(key, 11)
    base = jax.random.normal(key, (LAYERS, TOKENS, HEADS * HD), jnp.float32)
    return jnp.clip(base, -200.0, 200.0).astype(jnp.bfloat16)


def shard_levels(own_key, shape, shards, low, high):
    def one(position, shards_of):
        heights = jax.random.uniform(jax.random.fold_in(jax.random.fold_in(own_key, 6), position), (shards_of,), jnp.float32, low / len(shards), high / len(shards))
        return jnp.repeat(jnp.exp(heights), shape[position] // shards_of).reshape((-1,) + (1,) * (len(shape) - position - 1))

    factor_of = one(*shards[0])
    for cut in shards[1:]:
        factor_of = factor_of * one(*cut)
    return factor_of


def scatter_about(key, dims, deviation, limit, cuts=(), kind=jnp.bfloat16):
    factor_of = shard_levels(key, dims, cuts, -0.22, 0.18) if cuts else 1.0
    values = jax.random.normal(key, dims, jnp.float32) * deviation * factor_of
    return jnp.minimum(jnp.maximum(values, -limit), limit).astype(kind)


def setup_inputs(seed: int = 0) -> dict:
    key_of = jax.random.split(jax.random.key(seed), 6)
    rows40 = scatter_about(key_of[0], (TOKENS, D), 1.0, 6.0, ((0, 16), (1, 16)))
    queries = draw_queries(jax.random.fold_in(key_of[5], 71), 0)
    kv_weight = scatter_about(key_of[2], (LAYERS, D, KV_HEADS * 2 * HD), D ** -0.5, 0.0625, ((0, 4), (1, 16), (2, 4)))
    out_grad = scatter_about(key_of[3], (LAYERS, TOKENS, HEADS * HD), 1.0, 6.0, ((0, 4), (1, 16), (2, 4)))
    block_order = jax.random.permutation(key_of[4], SLOTS * N_SEQ).astype(jnp.int32)
    return dict(rows40=rows40, queries=queries, kv_weight=kv_weight, out_grad=out_grad, block_order=block_order)


def one_head(keys, values, visible, scale, pair):
    query_head, grad_head = pair
    raw = jnp.dot(query_head, keys.T, preferred_element_type=jnp.float32) * scale
    scores = jnp.where(visible, raw, -1e30)
    peak = jnp.max(scores, axis=1)
    expo = jnp.exp(scores - peak[:, None])
    total = jnp.sum(expo, axis=1)
    probs = expo / total[:, None]
    weights = probs.astype(jnp.bfloat16)
    output = jnp.dot(weights, values, preferred_element_type=jnp.float32).astype(jnp.bfloat16)
    delta = jnp.sum(grad_head.astype(jnp.float32) * output.astype(jnp.float32), axis=1)
    dprob = jnp.dot(grad_head, values.T, preferred_element_type=jnp.float32)
    dscore = (probs * (dprob - delta[:, None]) * scale).astype(jnp.bfloat16)
    dquery = jnp.dot(dscore, keys, preferred_element_type=jnp.float32).astype(jnp.bfloat16)
    dkey = jnp.dot(dscore.T, query_head, preferred_element_type=jnp.float32)
    dvalue = jnp.dot(weights.T, grad_head, preferred_element_type=jnp.float32)
    return output, dquery, dkey, dvalue


def reference(rows40, queries, kv_weight, out_grad, block_order):
    scale = HD ** -0.5
    half = TOK_DEV // SLOTS
    group = HEADS // KV_HEADS
    rows = jnp.arange(TOKENS, dtype=jnp.int32)
    pos = block_order[rows // half] * half + rows % half
    visible = pos[None, :] <= pos[:, None]
    attended_all = []
    qgrad_all = []
    wgrad_all = []
    for layer in range(LAYERS):
        kv = jnp.dot(rows40, kv_weight[layer], preferred_element_type=jnp.float32).astype(jnp.bfloat16)
        kv = kv.reshape(TOKENS, KV_HEADS, 2, HD)
        query = queries[layer].reshape(TOKENS, KV_HEADS, group, HD)
        grad = out_grad[layer].reshape(TOKENS, KV_HEADS, group, HD)
        outputs = []
        dqueries = []
        kv_grads = []
        for head in range(KV_HEADS):
            keys = kv[:, head, 0]
            values = kv[:, head, 1]
            output, dquery, dkey, dvalue = lax.map(
                partial(one_head, keys, values, visible, scale),
                (jnp.transpose(query[:, head], (1, 0, 2)), jnp.transpose(grad[:, head], (1, 0, 2))))
            outputs.append(jnp.transpose(output, (1, 0, 2)))
            dqueries.append(jnp.transpose(dquery, (1, 0, 2)))
            kv_grads.append(jnp.sum(dkey, axis=0).astype(jnp.bfloat16))
            kv_grads.append(jnp.sum(dvalue, axis=0).astype(jnp.bfloat16))
        attended_all.append(jnp.stack(outputs, axis=1).reshape(TOKENS, HEADS * HD))
        qgrad_all.append(jnp.stack(dqueries, axis=1).reshape(TOKENS, HEADS * HD))
        kv_grad = jnp.concatenate(kv_grads, axis=1)
        wgrad_all.append(jnp.dot(rows40.T, kv_grad, preferred_element_type=jnp.float32))
    return jnp.stack(attended_all), jnp.stack(qgrad_all), jnp.stack(wgrad_all)
```

```python
import functools

import jax
import jax.numpy as jnp
from jax import lax
import jax.experimental.pallas as pl
import jax.experimental.pallas.tpu as pltpu
from jax.sharding import PartitionSpec as P

HD = 128
SLOTS = 4
CHUNK = 256
VMEM_LIMIT = 60 * 2**20
MESH = pl.DeviceIdType.MESH
LOG2E = 1.4426950408889634


def contract(left, right, left_dim, right_dim):
    return lax.dot_general(
        left,
        right,
        (((left_dim,), (right_dim,)), ((), ())),
        preferred_element_type=jnp.float32,
    )


class Copies:
    def __init__(self, send_sem, recv_sem):
        self.send_sem = send_sem
        self.recv_sem = recv_sem
        self.count = 0
        self.started = []

    def slot(self):
        self.count += 1
        return self.count - 1

    def make(self, slot, src, dst, device):
        return pltpu.make_async_remote_copy(
            src_ref=src,
            dst_ref=dst,
            send_sem=self.send_sem.at[slot],
            recv_sem=self.recv_sem.at[slot],
            device_id=device,
            device_id_type=MESH,
        )

    def start(self, slot, src, dst, device):
        copy = self.make(slot, src, dst, device)
        copy.start()
        self.started.append(copy)

    def wait_recv(self, slot, buf, device):
        self.make(slot, buf, buf, device).wait_recv()

    def finish(self):
        for copy in self.started:
            copy.wait_send()


def place():
    sec = lax.axis_index("section")
    seq = lax.axis_index("seq")
    mp = lax.axis_index("mp")
    return sec, seq, mp


def greet(peers):
    barrier = pltpu.get_barrier_semaphore()
    for peer in peers:
        pl.semaphore_signal(barrier, inc=1, device_id=peer, device_id_type=MESH)
    pl.semaphore_wait(barrier, len(peers))


def seq_peers(sec, seq, mp):
    zhi = lax.rem(seq // 2, 2)
    core = lax.rem(seq, 2)
    across = (sec, seq + 2 - 4 * zhi, mp)
    other = (sec, seq + 1 - 2 * core, mp)
    along = {d: (sec, lax.rem(seq + 4 * d, 16), mp) for d in (1, 2, 3)}
    return across, other, along


class SeqGather:
    def __init__(self, copies, buf, sec, seq, mp):
        self.copies = copies
        self.buf = buf
        self.seq = seq
        self.across, self.other, self.along = seq_peers(sec, seq, mp)
        self.z_slot = copies.slot()
        self.y_slot = {(t, d): copies.slot() for t in (0, 1) for d in (1, 2, 3)}
        self.c_slot = {(t, d): copies.slot() for t in (0, 1) for d in (0, 1, 2, 3)}

    def index(self, t, d):
        own = lax.rem(self.seq + 16 - 4 * d, 16)
        if t == 0:
            return own
        return own + 2 - 4 * lax.rem(own // 2, 2)

    def send(self, slot, t, d, device):
        block = self.buf.at[self.index(t, d)]
        self.copies.start(slot, block, block, device)

    def begin(self):
        self.send(self.z_slot, 0, 0, self.across)
        for d in (1, 2, 3):
            self.send(self.y_slot[0, d], 0, 0, self.along[d])
        self.send(self.c_slot[0, 0], 0, 0, self.other)

    def relay_across(self):
        self.copies.wait_recv(self.z_slot, self.buf.at[0], self.across)
        for d in (1, 2, 3):
            self.send(self.y_slot[1, d], 1, 0, self.along[d])
        self.send(self.c_slot[1, 0], 1, 0, self.other)

    def relay_core(self, t, d):
        self.copies.wait_recv(self.y_slot[t, d], self.buf.at[0], self.along[d])
        self.send(self.c_slot[t, d], t, d, self.other)

    def end(self):
        for t in (0, 1):
            for d in (0, 1, 2, 3):
                self.copies.wait_recv(self.c_slot[t, d], self.buf.at[0], self.other)


def project_kernel(rows_ref, weight_ref, kv_ref, rows_all, weight_all, send_sem, recv_sem):
    sec, seq, mp = place()
    copies = Copies(send_sem, recv_sem)
    mp_peer = {d: (sec, seq, lax.rem(mp + d, 4)) for d in (1, 2, 3)}
    sec_peer = {d: (lax.rem(sec + d, 4), seq, mp) for d in (1, 2, 3)}
    across, other, along = seq_peers(sec, seq, mp)
    greet(
        [mp_peer[d] for d in (1, 2, 3)]
        + [sec_peer[d] for d in (1, 2, 3)]
        + [along[d] for d in (1, 2, 3)]
        + [across, other]
    )
    own = sec * 4 + mp
    rows_all[own] = rows_ref[...]
    weight_all[seq] = weight_ref[0]
    gather_w = SeqGather(copies, weight_all, sec, seq, mp)
    m_slot = {d: copies.slot() for d in (1, 2, 3)}
    x_slot = {(e, d): copies.slot() for e in (0, 1, 2, 3) for d in (1, 2, 3)}

    for d in (1, 2, 3):
        copies.start(m_slot[d], rows_all.at[own], rows_all.at[own], mp_peer[d])
    gather_w.begin()
    for d in (1, 2, 3):
        copies.start(x_slot[0, d], rows_all.at[own], rows_all.at[own], sec_peer[d])
    for e in (1, 3, 2):
        copies.wait_recv(m_slot[e], rows_all.at[0], mp_peer[e])
        block = sec * 4 + lax.rem(mp + 4 - e, 4)
        for d in (1, 2, 3):
            copies.start(x_slot[e, d], rows_all.at[block], rows_all.at[block], sec_peer[d])
        if e == 1:
            gather_w.relay_across()
    for t in (0, 1):
        for d in (1, 3, 2):
            gather_w.relay_core(t, d)
    for e in (0, 1, 3, 2):
        for d in (1, 3, 2):
            copies.wait_recv(x_slot[e, d], rows_all.at[0], sec_peer[d])
    gather_w.end()

    def term(f, total):
        return total + jnp.dot(
            rows_all[f], weight_all[f], preferred_element_type=jnp.float32
        )

    total = lax.fori_loop(0, 16, term, jnp.zeros(kv_ref.shape[1:], jnp.float32))
    kv_ref[seq] = total.astype(kv_ref.dtype)

    gather_kv = SeqGather(copies, kv_ref, sec, seq, mp)
    gather_kv.begin()
    gather_kv.relay_core(0, 1)
    gather_kv.relay_core(0, 3)
    gather_kv.relay_core(0, 2)
    gather_kv.relay_across()
    for d in (1, 3, 2):
        gather_kv.relay_core(1, d)
    gather_kv.end()
    copies.finish()


def project(rows, weight):
    tok, feat = rows.shape
    cols = weight.shape[2]
    sems = 45
    return pl.pallas_call(
        project_kernel,
        out_shape=jax.ShapeDtypeStruct((16, tok, cols), jnp.bfloat16),
        in_specs=[pl.BlockSpec(memory_space=pltpu.VMEM)] * 2,
        out_specs=pl.BlockSpec(memory_space=pltpu.VMEM),
        scratch_shapes=[
            pltpu.VMEM((16, tok, feat), jnp.bfloat16),
            pltpu.VMEM((16, feat, cols), jnp.bfloat16),
            pltpu.SemaphoreType.DMA((sems,)),
            pltpu.SemaphoreType.DMA((sems,)),
        ],
        compiler_params=pltpu.CompilerParams(
            collective_id=0, has_side_effects=True, vmem_limit_bytes=VMEM_LIMIT
        ),
        name="project",
    )(rows, weight)


def attention_kernel(
    order, q_ref, g_ref, kv_ref, att_ref, dq_ref, dkv_ref, kv_pos, kv_t, acc, score, prob
):
    seq = lax.axis_index("seq")
    half = q_ref.shape[0] // SLOTS
    group = q_ref.shape[1] // HD
    keys = kv_ref.shape[0]
    lanes = group * half
    scale = HD ** (-0.5)
    rate = scale * LOG2E

    def rows_at(start, size):
        return pl.ds(pl.multiple_of(start, 16), size)

    def by_position(r, carry):
        kv_pos[rows_at(order[r] * half, half), :] = kv_ref[rows_at(r * half, half), :]
        return carry

    lax.fori_loop(0, keys // half, by_position, 0)

    def turn(j, carry):
        kv_t[j] = kv_pos[rows_at(j * CHUNK, CHUNK), :].T
        acc[rows_at(j * CHUNK, CHUNK), :] = jnp.zeros((CHUNK, 2 * HD), jnp.float32)
        return carry

    lax.fori_loop(0, keys // CHUNK, turn, 0)

    def slot(i, carry):
        first = order[seq * SLOTS + i] * half
        rows = rows_at(i * half, half)
        q = jnp.concatenate([q_ref[rows, h * HD : (h + 1) * HD] for h in range(group)], axis=0)
        g = jnp.concatenate([g_ref[rows, h * HD : (h + 1) * HD] for h in range(group)], axis=0)
        whole = first // CHUNK
        some = (first + half + CHUNK - 1) // CHUNK

        def scores(masked):
            def step(j, peak):
                raw = contract(kv_pos[rows_at(j * CHUNK, CHUNK), :HD], q, 1, 1)
                if masked:
                    key = j * CHUNK + lax.broadcasted_iota(jnp.int32, raw.shape, 0)
                    query = first + lax.rem(
                        lax.broadcasted_iota(jnp.int32, raw.shape, 1), half
                    )
                    raw = jnp.where(key <= query, raw, -1e30)
                score[rows_at(j * CHUNK, CHUNK), :] = raw
                return jnp.maximum(peak, jnp.max(raw.reshape(CHUNK // 8, 8, lanes), axis=0))

            return step

        peak = jnp.full((8, lanes), -1e30, jnp.float32)
        peak = lax.fori_loop(0, whole, scores(False), peak)
        peak = lax.fori_loop(whole, some, scores(True), peak)
        peak = jnp.max(peak, axis=0, keepdims=True)

        def weigh(j, total):
            at = rows_at(j * CHUNK, CHUNK)
            expo = jnp.exp2((score[at, :] - peak) * rate)
            score[at, :] = expo
            return total + jnp.sum(expo.reshape(CHUNK // 8, 8, lanes), axis=0)

        total = lax.fori_loop(0, some, weigh, jnp.zeros((8, lanes), jnp.float32))
        part = 1.0 / jnp.sum(total, axis=0, keepdims=True)

        def attend(j, out):
            at = rows_at(j * CHUNK, CHUNK)
            weights = (score[at, :] * part).astype(jnp.bfloat16)
            prob[at, :] = weights
            return out + jnp.dot(kv_t[j, HD:], weights, preferred_element_type=jnp.float32)

        out = lax.fori_loop(0, some, attend, jnp.zeros((HD, lanes), jnp.float32))
        out = out.astype(jnp.bfloat16).astype(jnp.float32)
        delta = jnp.sum(g.astype(jnp.float32).T * out, axis=0, keepdims=True)
        out = out.T.astype(jnp.bfloat16)
        for h in range(group):
            att_ref[rows, h * HD : (h + 1) * HD] = out[h * half : (h + 1) * half, :]
        part_scaled = part * scale

        def back(j, dquery):
            at = rows_at(j * CHUNK, CHUNK)
            dprob = contract(kv_pos[at, HD:], g, 1, 1)
            dscore = (score[at, :] * part_scaled * (dprob - delta)).astype(jnp.bfloat16)
            acc[at, :HD] += jnp.dot(dscore, q, preferred_element_type=jnp.float32)
            acc[at, HD:] += jnp.dot(prob[at, :], g, preferred_element_type=jnp.float32)
            return dquery + jnp.dot(kv_t[j, :HD], dscore, preferred_element_type=jnp.float32)

        dquery = lax.fori_loop(0, some, back, jnp.zeros((HD, lanes), jnp.float32))
        dquery = dquery.T.astype(jnp.bfloat16)
        for h in range(group):
            dq_ref[rows, h * HD : (h + 1) * HD] = dquery[h * half : (h + 1) * half, :]
        return carry

    lax.fori_loop(0, SLOTS, slot, 0)

    def by_token(r, carry):
        dkv_ref[rows_at(r * half, half), :] = acc[rows_at(order[r] * half, half), :].astype(
            jnp.bfloat16
        )
        return carry

    lax.fori_loop(0, keys // half, by_token, 0)


def attention(order, queries, out_grad, kv):
    tok, cols = queries.shape
    keys = kv.shape[0]
    lanes = cols // HD * (tok // SLOTS)
    vmem = pl.BlockSpec(memory_space=pltpu.VMEM)
    return pl.pallas_call(
        attention_kernel,
        out_shape=(
            jax.ShapeDtypeStruct((tok, cols), jnp.bfloat16),
            jax.ShapeDtypeStruct((tok, cols), jnp.bfloat16),
            jax.ShapeDtypeStruct((keys, 2 * HD), jnp.bfloat16),
        ),
        in_specs=[pl.BlockSpec(memory_space=pltpu.SMEM), vmem, vmem, vmem],
        out_specs=(vmem, vmem, vmem),
        scratch_shapes=[
            pltpu.VMEM((keys, 2 * HD), jnp.bfloat16),
            pltpu.VMEM((keys // CHUNK, 2 * HD, CHUNK), jnp.bfloat16),
            pltpu.VMEM((keys, 2 * HD), jnp.float32),
            pltpu.VMEM((keys, lanes), jnp.float32),
            pltpu.VMEM((keys, lanes), jnp.bfloat16),
        ],
        compiler_params=pltpu.CompilerParams(vmem_limit_bytes=VMEM_LIMIT),
        name="attention",
    )(order, queries, out_grad, kv)


def weight_grad_kernel(
    rows_ref, dkv_ref, out_ref, rows_t, core_in, y_out, y_in, z_out, z_in, grad, send_sem, recv_sem
):
    sec, seq, mp = place()
    copies = Copies(send_sem, recv_sem)
    yy = seq // 4
    core = lax.rem(seq, 2)
    across, other, along = seq_peers(sec, seq, mp)
    sec_peer = {d: (lax.rem(sec + d, 4), seq, mp) for d in (1, 2, 3)}
    feature = sec * 4 + mp
    diagonal = seq == feature
    to_peer = {d: (seq // 4, feature, lax.rem(mp + d, 4)) for d in (0, 1, 2, 3)}
    from_peer = {j: (seq // 4, sec * 4 + j, lax.rem(seq, 4)) for j in (0, 1, 2, 3)}

    barrier = pltpu.get_barrier_semaphore()
    fixed = [sec_peer[d] for d in (1, 2, 3)] + [along[d] for d in (1, 2, 3)] + [across, other]
    for peer in fixed:
        pl.semaphore_signal(barrier, inc=1, device_id=peer, device_id_type=MESH)
    for j in (0, 1, 2, 3):
        away = jnp.logical_not(jnp.logical_and(diagonal, mp == j))

        @pl.when(away)
        def _():
            pl.semaphore_signal(barrier, inc=1, device_id=from_peer[j], device_id_type=MESH)

    pl.semaphore_wait(barrier, len(fixed) + 4 - diagonal.astype(jnp.int32))

    first_slot = [copies.slot() for _ in range(4)]
    x_slot = {(j, d): copies.slot() for j in range(4) for d in (1, 2, 3)}
    core_slot = [copies.slot() for _ in range(4)]
    y_slot = {d: copies.slot() for d in (1, 2, 3)}
    z_slot = copies.slot()
    ag_slot = {d: copies.slot() for d in (1, 2, 3)}
    cg_slot = {d: copies.slot() for d in (0, 1, 2, 3)}

    for d in (1, 2, 3, 0):
        yt = lax.rem(yy + d, 4)
        copies.start(core_slot[d], dkv_ref.at[yt, :, 1 - core], core_in.at[d], other)

    def first_copy(d):
        return pltpu.make_async_remote_copy(
            src_ref=rows_ref,
            dst_ref=rows_t.at[seq],
            send_sem=send_sem.at[first_slot[d]],
            recv_sem=recv_sem.at[first_slot[0] + lax.rem(seq, 4)],
            device_id=to_peer[d],
            device_id_type=MESH,
        )

    for d in (1, 2, 3):
        first_copy(d).start()

    @pl.when(diagonal)
    def _():
        rows_t[seq] = rows_ref[...]

    @pl.when(jnp.logical_not(diagonal))
    def _():
        first_copy(0).start()

    for d in (1, 2, 3):
        yt = lax.rem(yy + d, 4)
        copies.wait_recv(core_slot[d], core_in.at[d], other)
        y_out[d - 1] = (
            dkv_ref[yt, :, core].astype(jnp.float32) + core_in[d].astype(jnp.float32)
        ).astype(jnp.bfloat16)
        copies.start(y_slot[d], y_out.at[d - 1], y_in.at[d - 1], along[d])
    copies.wait_recv(core_slot[0], core_in.at[0], other)

    for j in range(4):
        @pl.when(jnp.logical_not(jnp.logical_and(diagonal, mp == j)))
        def _():
            copies.wait_recv(first_slot[j], rows_t.at[0], from_peer[j])

        block = rows_t.at[sec * 4 + j]
        for d in (1, 2, 3):
            copies.start(x_slot[j, d], block, block, sec_peer[d])

    for d in (1, 2, 3):
        copies.wait_recv(y_slot[d], y_in.at[d - 1], along[d])
    z_out[...] = (
        dkv_ref[yy, :, core].astype(jnp.float32)
        + core_in[0].astype(jnp.float32)
        + y_in[0].astype(jnp.float32)
        + y_in[1].astype(jnp.float32)
        + y_in[2].astype(jnp.float32)
    ).astype(jnp.bfloat16)
    copies.start(z_slot, z_out, z_in, across)
    copies.wait_recv(z_slot, z_in, across)
    grad[yy, :, core] = (
        z_out[...].astype(jnp.float32) + z_in[...].astype(jnp.float32)
    ).astype(jnp.bfloat16)
    own = grad.at[yy, :, core]
    for d in (1, 2, 3):
        copies.start(ag_slot[d], own, own, along[d])
    copies.start(cg_slot[0], own, own, other)
    for d in (1, 3, 2):
        block = grad.at[lax.rem(yy + 4 - d, 4), :, core]
        copies.wait_recv(ag_slot[d], block, along[d])
        copies.start(cg_slot[d], block, block, other)
    for d in (0, 1, 3, 2):
        copies.wait_recv(cg_slot[d], grad.at[0, :, 0], other)
    for j in range(4):
        for d in (1, 3, 2):
            copies.wait_recv(x_slot[j, d], rows_t.at[0], sec_peer[d])

    out_ref[...] = jnp.zeros_like(out_ref)

    def term(t, carry):
        block = grad[t // 4, lax.rem(t // 2, 2), lax.rem(t, 2)]
        out_ref[...] += contract(rows_t[t], block, 0, 0)
        return carry

    lax.fori_loop(0, 16, term, 0)

    for d in (1, 2, 3):
        first_copy(d).wait_send()

    @pl.when(jnp.logical_not(diagonal))
    def _():
        first_copy(0).wait_send()

    copies.finish()


def weight_grad(rows, dkv):
    tok, feat = rows.shape
    cols = dkv.shape[1]
    sems = 40
    vmem = pl.BlockSpec(memory_space=pltpu.VMEM)
    half = (2, tok, cols)
    return pl.pallas_call(
        weight_grad_kernel,
        out_shape=jax.ShapeDtypeStruct((feat, cols), jnp.float32),
        in_specs=[vmem, vmem],
        out_specs=vmem,
        scratch_shapes=[
            pltpu.VMEM((16, tok, feat), jnp.bfloat16),
            pltpu.VMEM((4,) + half, jnp.bfloat16),
            pltpu.VMEM((3,) + half, jnp.bfloat16),
            pltpu.VMEM((3,) + half, jnp.bfloat16),
            pltpu.VMEM(half, jnp.bfloat16),
            pltpu.VMEM(half, jnp.bfloat16),
            pltpu.VMEM((4, 2, 2, tok, cols), jnp.bfloat16),
            pltpu.SemaphoreType.DMA((sems,)),
            pltpu.SemaphoreType.DMA((sems,)),
        ],
        compiler_params=pltpu.CompilerParams(
            collective_id=1, has_side_effects=True, vmem_limit_bytes=VMEM_LIMIT
        ),
        name="weight_grad",
    )(rows, dkv.reshape(4, 2, 2, tok, cols))


def body(rows40, queries, kv_weight, out_grad, block_order):
    tok = rows40.shape[0]
    kv = project(rows40, kv_weight)
    attended, query_grad, dkv = attention(
        block_order, queries[0], out_grad[0], kv.reshape(16 * tok, 2 * HD)
    )
    grad = weight_grad(rows40, dkv)
    return (attended[None], query_grad[None], grad[None])


def solution(mesh):
    return jax.shard_map(
        body,
        mesh=mesh,
        in_specs=(
            P("seq", ("section", "mp")),
            P("section", "seq", "mp"),
            P("section", "seq", "mp"),
            P("section", "seq", "mp"),
            P(),
        ),
        out_specs=(P("section", "seq", "mp"), P("section", "seq", "mp"), P("section", "seq", "mp")),
        check_vma=False,
    )
```

```python
import functools

import jax
import jax.numpy as jnp
from jax import lax
import jax.experimental.pallas as pl
import jax.experimental.pallas.tpu as pltpu
from jax.sharding import PartitionSpec as P

HD = 128
SLOTS = 4
PIECES = 4
VMEM_LIMIT = 60 * 2**20
MESH = pl.DeviceIdType.MESH
LOG2E = 1.4426950408889634


def contract(left, right, left_dim, right_dim):
    return lax.dot_general(
        left,
        right,
        (((left_dim,), (right_dim,)), ((), ())),
        preferred_element_type=jnp.float32,
    )


class Copies:
    def __init__(self, send_sem, recv_sem):
        self.send_sem = send_sem
        self.recv_sem = recv_sem
        self.count = 0
        self.started = []

    def slot(self):
        self.count += 1
        return self.count - 1

    def make(self, slot, src, dst, device):
        return pltpu.make_async_remote_copy(
            src_ref=src,
            dst_ref=dst,
            send_sem=self.send_sem.at[slot],
            recv_sem=self.recv_sem.at[slot],
            device_id=device,
            device_id_type=MESH,
        )

    def start(self, slot, src, dst, device):
        copy = self.make(slot, src, dst, device)
        copy.start()
        self.started.append(copy)

    def wait_recv(self, slot, buf, device):
        self.make(slot, buf, buf, device).wait_recv()

    def finish(self):
        for copy in self.started:
            copy.wait_send()


def place():
    sec = lax.axis_index("section")
    seq = lax.axis_index("seq")
    mp = lax.axis_index("mp")
    return sec, seq, mp


def greet(peers):
    barrier = pltpu.get_barrier_semaphore()
    for peer in peers:
        pl.semaphore_signal(barrier, inc=1, device_id=peer, device_id_type=MESH)
    pl.semaphore_wait(barrier, len(peers))


def seq_peers(sec, seq, mp):
    zhi = lax.rem(seq // 2, 2)
    core = lax.rem(seq, 2)
    across = (sec, seq + 2 - 4 * zhi, mp)
    other = (sec, seq + 1 - 2 * core, mp)
    along = {d: (sec, lax.rem(seq + 4 * d, 16), mp) for d in (1, 2, 3)}
    return across, other, along


class SeqGather:
    def __init__(self, copies, buf, sec, seq, mp):
        self.copies = copies
        self.buf = buf
        self.seq = seq
        self.across, self.other, self.along = seq_peers(sec, seq, mp)
        self.z_slot = copies.slot()
        self.y_slot = {(t, d): copies.slot() for t in (0, 1) for d in (1, 2, 3)}
        self.c_slot = {(t, d): copies.slot() for t in (0, 1) for d in (0, 1, 2, 3)}

    def index(self, t, d):
        own = lax.rem(self.seq + 16 - 4 * d, 16)
        if t == 0:
            return own
        return own + 2 - 4 * lax.rem(own // 2, 2)

    def send(self, slot, t, d, device):
        block = self.buf.at[self.index(t, d)]
        self.copies.start(slot, block, block, device)

    def begin_far(self):
        self.send(self.z_slot, 0, 0, self.across)

    def begin_near(self):
        for d in (1, 3, 2):
            self.send(self.y_slot[0, d], 0, 0, self.along[d])
        self.send(self.c_slot[0, 0], 0, 0, self.other)

    def relay_across(self):
        self.copies.wait_recv(self.z_slot, self.buf.at[0], self.across)
        for d in (1, 3, 2):
            self.send(self.y_slot[1, d], 1, 0, self.along[d])
        self.send(self.c_slot[1, 0], 1, 0, self.other)

    def relay_core(self, t, d):
        self.copies.wait_recv(self.y_slot[t, d], self.buf.at[0], self.along[d])
        self.send(self.c_slot[t, d], t, d, self.other)

    def end(self):
        for t in (0, 1):
            for d in (0, 1, 2, 3):
                self.copies.wait_recv(self.c_slot[t, d], self.buf.at[0], self.other)


def project_kernel(
    rows_ref, weight_ref, kv_ref, turned_ref, rows_all, weight_all, send_sem, recv_sem
):
    sec, seq, mp = place()
    copies = Copies(send_sem, recv_sem)
    mp_peer = {d: (sec, seq, lax.rem(mp + d, 4)) for d in (1, 2, 3)}
    sec_peer = {d: (lax.rem(sec + d, 4), seq, mp) for d in (1, 2, 3)}
    across, other, along = seq_peers(sec, seq, mp)
    own = sec * 4 + mp
    diagonal = seq == own
    mirror = (seq // 4, own, lax.rem(seq, 4))

    barrier = pltpu.get_barrier_semaphore()
    peers = (
        [mp_peer[d] for d in (1, 2, 3)]
        + [sec_peer[d] for d in (1, 2, 3)]
        + [along[d] for d in (1, 2, 3)]
        + [across, other]
    )
    for peer in peers:
        pl.semaphore_signal(barrier, inc=1, device_id=peer, device_id_type=MESH)

    @pl.when(jnp.logical_not(diagonal))
    def _():
        pl.semaphore_signal(barrier, inc=1, device_id=mirror, device_id_type=MESH)

    rows_all[own] = rows_ref[...]
    weight_all[seq] = weight_ref[0]
    pl.semaphore_wait(barrier, len(peers) + 1 - diagonal.astype(jnp.int32))

    gather_w = SeqGather(copies, weight_all, sec, seq, mp)
    gather_kv = SeqGather(copies, kv_ref, sec, seq, mp)
    m_slot = {d: copies.slot() for d in (1, 2, 3)}
    x_slot = {(e, d): copies.slot() for e in (0, 1, 2, 3) for d in (1, 2, 3)}
    turn_slot = copies.slot()

    def pass_on(e):
        block = rows_all.at[sec * 4 + lax.rem(mp + 4 - e, 4)]
        if e:
            copies.wait_recv(m_slot[e], block, mp_peer[e])
        for d in (1, 3, 2):
            copies.start(x_slot[e, d], block, block, sec_peer[d])

    block = rows_all.at[own]
    for d in (1, 3):
        copies.start(m_slot[d], block, block, mp_peer[d])
    pass_on(0)
    gather_w.begin_near()
    pass_on(1)
    gather_w.begin_far()
    pass_on(3)
    copies.start(m_slot[2], block, block, mp_peer[2])
    for d in (1, 3, 2):
        gather_w.relay_core(0, d)
    gather_w.relay_across()
    pass_on(2)
    for d in (1, 3, 2):
        gather_w.relay_core(1, d)
    for e in (0, 1, 3, 2):
        for d in (1, 3, 2):
            copies.wait_recv(x_slot[e, d], rows_all.at[0], sec_peer[d])

    turn = copies.make(turn_slot, rows_all.at[own], turned_ref, mirror)

    @pl.when(diagonal)
    def _():
        turned_ref[...] = rows_ref[...]

    @pl.when(jnp.logical_not(diagonal))
    def _():
        turn.start()

    gather_w.end()

    def term(f, total):
        return total + jnp.dot(
            rows_all[f], weight_all[f], preferred_element_type=jnp.float32
        )

    total = lax.fori_loop(0, 16, term, jnp.zeros(kv_ref.shape[1:], jnp.float32))
    kv_ref[seq] = total.astype(kv_ref.dtype)

    gather_kv.begin_far()
    gather_kv.begin_near()
    for d in (1, 3, 2):
        gather_kv.relay_core(0, d)
    gather_kv.relay_across()
    for d in (1, 3, 2):
        gather_kv.relay_core(1, d)
    gather_kv.end()

    @pl.when(jnp.logical_not(diagonal))
    def _():
        turn.wait()

    copies.finish()


def project(rows, weight):
    tok, feat = rows.shape
    cols = weight.shape[2]
    sems = 46
    vmem = pl.BlockSpec(memory_space=pltpu.VMEM)
    return pl.pallas_call(
        project_kernel,
        out_shape=(
            jax.ShapeDtypeStruct((16, tok, cols), jnp.bfloat16),
            jax.ShapeDtypeStruct((tok, feat), jnp.bfloat16),
        ),
        in_specs=[vmem, vmem],
        out_specs=(vmem, vmem),
        scratch_shapes=[
            pltpu.VMEM((16, tok, feat), jnp.bfloat16),
            pltpu.VMEM((16, feat, cols), jnp.bfloat16),
            pltpu.SemaphoreType.DMA((sems,)),
            pltpu.SemaphoreType.DMA((sems,)),
        ],
        compiler_params=pltpu.CompilerParams(
            collective_id=0, has_side_effects=True, vmem_limit_bytes=VMEM_LIMIT
        ),
        name="project",
    )(rows, weight)


def attention_kernel(
    order,
    q_ref,
    g_ref,
    kv_ref,
    rows_ref,
    att_ref,
    dq_ref,
    out_ref,
    q_all,
    g_all,
    kv_t,
    score,
    prob,
    dscore,
    dquery,
    stats,
    rows_t,
    acc,
    keep,
    core_out,
    core_in,
    y_out,
    y_in,
    z_out,
    z_in,
    grad,
    send_sem,
    recv_sem,
):
    sec, seq, mp = place()
    copies = Copies(send_sem, recv_sem)
    yy = seq // 4
    core = lax.rem(seq, 2)
    across, other, along = seq_peers(sec, seq, mp)
    sec_peer = {d: (lax.rem(sec + d, 4), seq, mp) for d in (1, 2, 3)}
    mp_peer = {d: (sec, seq, lax.rem(mp + d, 4)) for d in (1, 2, 3)}
    greet(
        [mp_peer[d] for d in (1, 2, 3)]
        + [sec_peer[d] for d in (1, 2, 3)]
        + [along[d] for d in (1, 2, 3)]
        + [across, other]
    )

    m_slot = {d: copies.slot() for d in (1, 2, 3)}
    x_slot = {(e, d): copies.slot() for e in range(4) for d in (1, 2, 3)}
    core_slot = [copies.slot() for _ in range(4)]
    y_slot = {d: copies.slot() for d in (1, 2, 3)}
    z_slot = [copies.slot() for _ in range(PIECES)]
    ag_slot = {(p, d): copies.slot() for p in range(PIECES) for d in (1, 2, 3)}
    cg_slot = {(p, d): copies.slot() for p in range(PIECES) for d in (0, 1, 2, 3)}

    tok = q_ref.shape[0]
    half = tok // SLOTS
    group = q_ref.shape[1] // HD
    lanes = group * half
    part_rows = 4 * tok
    scale = HD ** (-0.5)
    rate = scale * LOG2E

    def token_block(t):
        return rows_t.at[t // 2, pl.ds(pl.multiple_of(lax.rem(t, 2) * tok, 16), tok), :]

    def pass_on(e):
        block = token_block(sec * 4 + lax.rem(mp + 4 - e, 4))
        if e:
            copies.wait_recv(m_slot[e], block, mp_peer[e])
        for d in (1, 3, 2):
            copies.start(x_slot[e, d], block, block, sec_peer[d])

    token_block(sec * 4 + mp)[...] = rows_ref[...]
    for d in (1, 3, 2):
        block = token_block(sec * 4 + mp)
        copies.start(m_slot[d], block, block, mp_peer[d])
    pass_on(0)

    def lane(i):
        return slice(i * lanes, (i + 1) * lanes)

    for i in range(SLOTS):
        for h in range(group):
            at = i * lanes + h * half
            rows = slice(i * half, (i + 1) * half)
            q_all[at : at + half, :] = q_ref[rows, h * HD : (h + 1) * HD]
            g_all[at : at + half, :] = g_ref[rows, h * HD : (h + 1) * HD]
    for j in range(4):
        kv_t[j] = kv_ref[j * part_rows : (j + 1) * part_rows, :].T

    for i in range(SLOTS):
        skew = lax.broadcasted_iota(jnp.int32, (half, lanes), 0) - lax.rem(
            lax.broadcasted_iota(jnp.int32, (half, lanes), 1), half
        )
        here = order[seq * SLOTS + i]
        peak = jnp.full((8, lanes), -1e30, jnp.float32)
        for j in range(4):
            raw = contract(
                kv_ref[j * part_rows : (j + 1) * part_rows, :HD], q_all[lane(i), :], 1, 1
            )
            for b in range(part_rows // half):
                ahead = (here - order[j * (part_rows // half) + b]) * half
                seen = jnp.where(skew <= ahead, raw[b * half : (b + 1) * half, :], -1e30)
                at = j * part_rows + b * half
                score[at : at + half, lane(i)] = seen
                peak = jnp.maximum(peak, jnp.max(seen.reshape(half // 8, 8, lanes), axis=0))
        peak = jnp.max(peak, axis=0, keepdims=True)
        total = jnp.zeros((8, lanes), jnp.float32)
        for j in range(4):
            at = slice(j * part_rows, (j + 1) * part_rows)
            expo = jnp.exp2((score[at, lane(i)] - peak) * rate)
            score[at, lane(i)] = expo
            total += jnp.sum(expo.reshape(part_rows // 8, 8, lanes), axis=0)
        part = 1.0 / jnp.sum(total, axis=0, keepdims=True)
        out = jnp.zeros((HD, lanes), jnp.float32)
        for j in range(4):
            at = slice(j * part_rows, (j + 1) * part_rows)
            weights = (score[at, lane(i)] * part).astype(jnp.bfloat16)
            prob[at, lane(i)] = weights
            out += jnp.dot(kv_t[j, HD:], weights, preferred_element_type=jnp.float32)
        out = out.astype(jnp.bfloat16).astype(jnp.float32)
        delta = jnp.sum(g_all[lane(i), :].astype(jnp.float32).T * out, axis=0, keepdims=True)
        stats[0, :, lane(i)] = jnp.broadcast_to(delta, (8, lanes))
        stats[1, :, lane(i)] = jnp.broadcast_to(part * scale, (8, lanes))
        out = out.T.astype(jnp.bfloat16)
        for h in range(group):
            att_ref[i * half : (i + 1) * half, h * HD : (h + 1) * HD] = out[
                h * half : (h + 1) * half, :
            ]
        if i == 1:
            pass_on(1)
        if i == 2:
            pass_on(3)

    def back(d):
        yt = lax.rem(yy + d, 4)
        rows = pl.ds(pl.multiple_of(yt * part_rows, 16), part_rows)
        for i in range(SLOTS):
            dprob = contract(kv_ref[rows, HD:], g_all[lane(i), :], 1, 1)
            dscore[:, lane(i)] = (
                score[rows, lane(i)]
                * stats[1, :1, lane(i)]
                * (dprob - stats[0, :1, lane(i)])
            ).astype(jnp.bfloat16)
        dkey = jnp.dot(dscore[...], q_all[...], preferred_element_type=jnp.float32)
        dvalue = jnp.dot(prob[rows, :], g_all[...], preferred_element_type=jnp.float32)
        acc[..., :HD] = dkey.reshape(2, 2, tok, HD)
        acc[..., HD:] = dvalue.reshape(2, 2, tok, HD)
        core_out[d] = acc[:, 1 - core].astype(jnp.bfloat16)
        copies.start(core_slot[d], core_out.at[d], core_in.at[d], other)
        keep[d] = acc[:, core]
        more = jnp.dot(kv_t[yt, :HD], dscore[...], preferred_element_type=jnp.float32)
        if d == 2:
            dquery[...] = more
        else:
            dquery[...] += more

    def send_along(d):
        copies.wait_recv(core_slot[d], core_in.at[d], other)
        y_out[d - 1] = (keep[d] + core_in[d].astype(jnp.float32)).astype(jnp.bfloat16)
        copies.start(y_slot[d], y_out.at[d - 1], y_in.at[d - 1], along[d])

    back(2)
    back(1)
    send_along(2)
    pass_on(2)
    back(3)
    send_along(1)
    back(0)
    send_along(3)
    for i in range(SLOTS):
        turned = dquery[:, lane(i)].T.astype(jnp.bfloat16)
        for h in range(group):
            dq_ref[i * half : (i + 1) * half, h * HD : (h + 1) * HD] = turned[
                h * half : (h + 1) * half, :
            ]
    copies.wait_recv(core_slot[0], core_in.at[0], other)
    for d in (1, 3, 2):
        copies.wait_recv(y_slot[d], y_in.at[d - 1], along[d])

    piece = tok // PIECES

    def piece_rows(p):
        return slice(p * piece, (p + 1) * piece)

    for p in range(PIECES):
        rows = piece_rows(p)
        total = keep[0, :, rows] + core_in[0, :, rows].astype(jnp.float32)
        for d in (1, 2, 3):
            total += y_in[d - 1, :, rows].astype(jnp.float32)
        z_out[p] = total.astype(jnp.bfloat16)
        copies.start(z_slot[p], z_out.at[p], z_in.at[p], across)
    for p in range(PIECES):
        copies.wait_recv(z_slot[p], z_in.at[p], across)
        grad[yy, :, core, piece_rows(p)] = (
            z_out[p].astype(jnp.float32) + z_in[p].astype(jnp.float32)
        ).astype(jnp.bfloat16)
        own = grad.at[yy, :, core, piece_rows(p)]
        for d in (1, 3, 2):
            copies.start(ag_slot[p, d], own, own, along[d])
        copies.start(cg_slot[p, 0], own, own, other)
    for p in range(PIECES):
        for d in (1, 3, 2):
            block = grad.at[lax.rem(yy + 4 - d, 4), :, core, piece_rows(p)]
            copies.wait_recv(ag_slot[p, d], block, along[d])
            copies.start(cg_slot[p, d], block, block, other)
    for j in range(4):
        for d in (1, 3, 2):
            copies.wait_recv(x_slot[j, d], token_block(0), sec_peer[d])
    for p in range(PIECES):
        for d in (0, 1, 3, 2):
            copies.wait_recv(cg_slot[p, d], grad.at[0, :, 0, piece_rows(p)], other)

    result = jnp.zeros(out_ref.shape, jnp.float32)
    for k in range(8):
        block = grad[k // 2, k % 2].reshape(2 * tok, 2 * HD)
        result += contract(rows_t[k], block, 0, 0)
    out_ref[...] = result

    copies.finish()


def attention(order, queries, out_grad, kv, rows):
    tok, cols = queries.shape
    feat = rows.shape[1]
    keys = kv.shape[0]
    lanes = cols // HD * tok
    sems = 3 + 12 + 4 + 3 + PIECES * 8
    vmem = pl.BlockSpec(memory_space=pltpu.VMEM)
    half = (2, tok, 2 * HD)
    pieces = (PIECES, 2, tok // PIECES, 2 * HD)
    return pl.pallas_call(
        attention_kernel,
        out_shape=(
            jax.ShapeDtypeStruct((tok, cols), jnp.bfloat16),
            jax.ShapeDtypeStruct((tok, cols), jnp.bfloat16),
            jax.ShapeDtypeStruct((feat, 2 * HD), jnp.float32),
        ),
        in_specs=[pl.BlockSpec(memory_space=pltpu.SMEM), vmem, vmem, vmem, vmem],
        out_specs=(vmem, vmem, vmem),
        scratch_shapes=[
            pltpu.VMEM((lanes, HD), jnp.bfloat16),
            pltpu.VMEM((lanes, HD), jnp.bfloat16),
            pltpu.VMEM((4, 2 * HD, keys // 4), jnp.bfloat16),
            pltpu.VMEM((keys, lanes), jnp.float32),
            pltpu.VMEM((keys, lanes), jnp.bfloat16),
            pltpu.VMEM((keys // 4, lanes), jnp.bfloat16),
            pltpu.VMEM((HD, lanes), jnp.float32),
            pltpu.VMEM((2, 8, lanes), jnp.float32),
            pltpu.VMEM((8, 2 * tok, feat), jnp.bfloat16),
            pltpu.VMEM((2,) + half, jnp.float32),
            pltpu.VMEM((4,) + half, jnp.float32),
            pltpu.VMEM((4,) + half, jnp.bfloat16),
            pltpu.VMEM((4,) + half, jnp.bfloat16),
            pltpu.VMEM((3,) + half, jnp.bfloat16),
            pltpu.VMEM((3,) + half, jnp.bfloat16),
            pltpu.VMEM(pieces, jnp.bfloat16),
            pltpu.VMEM(pieces, jnp.bfloat16),
            pltpu.VMEM((4, 2) + half, jnp.bfloat16),
            pltpu.SemaphoreType.DMA((sems,)),
            pltpu.SemaphoreType.DMA((sems,)),
        ],
        compiler_params=pltpu.CompilerParams(
            collective_id=1, has_side_effects=True, vmem_limit_bytes=VMEM_LIMIT
        ),
        name="attention",
    )(order, queries, out_grad, kv, rows)


def body(rows40, queries, kv_weight, out_grad, block_order):
    tok = rows40.shape[0]
    kv, turned = project(rows40, kv_weight)
    attended, query_grad, grad = attention(
        block_order, queries[0], out_grad[0], kv.reshape(16 * tok, 2 * HD), turned
    )
    return (attended[None], query_grad[None], grad[None])


def solution(mesh):
    return jax.shard_map(
        body,
        mesh=mesh,
        in_specs=(
            P("seq", ("section", "mp")),
            P("section", "seq", "mp"),
            P("section", "seq", "mp"),
            P("section", "seq", "mp"),
            P(),
        ),
        out_specs=(P("section", "seq", "mp"), P("section", "seq", "mp"), P("section", "seq", "mp")),
        check_vma=False,
    )
```

```python
import functools

import jax
import jax.numpy as jnp
from jax import lax
import jax.experimental.pallas as pl
import jax.experimental.pallas.tpu as pltpu
from jax.sharding import PartitionSpec as P

HD = 128
SLOTS = 4
PIECES = 4
VMEM_LIMIT = 60 * 2**20
MESH = pl.DeviceIdType.MESH
LOG2E = 1.4426950408889634


def contract(left, right, left_dim, right_dim):
    return lax.dot_general(
        left,
        right,
        (((left_dim,), (right_dim,)), ((), ())),
        preferred_element_type=jnp.float32,
    )


class Copies:
    def __init__(self, send_sem, recv_sem):
        self.send_sem = send_sem
        self.recv_sem = recv_sem
        self.count = 0
        self.started = []

    def slot(self):
        self.count += 1
        return self.count - 1

    def make(self, slot, src, dst, device):
        return pltpu.make_async_remote_copy(
            src_ref=src,
            dst_ref=dst,
            send_sem=self.send_sem.at[slot],
            recv_sem=self.recv_sem.at[slot],
            device_id=device,
            device_id_type=MESH,
        )

    def start(self, slot, src, dst, device):
        copy = self.make(slot, src, dst, device)
        copy.start()
        self.started.append(copy)

    def wait_recv(self, slot, buf, device):
        self.make(slot, buf, buf, device).wait_recv()

    def finish(self):
        for copy in self.started:
            copy.wait_send()


def place():
    sec = lax.axis_index("section")
    seq = lax.axis_index("seq")
    mp = lax.axis_index("mp")
    return sec, seq, mp


def greet(peers):
    barrier = pltpu.get_barrier_semaphore()
    for peer in peers:
        pl.semaphore_signal(barrier, inc=1, device_id=peer, device_id_type=MESH)
    pl.semaphore_wait(barrier, len(peers))


def seq_peers(sec, seq, mp):
    zhi = lax.rem(seq // 2, 2)
    core = lax.rem(seq, 2)
    across = (sec, seq + 2 - 4 * zhi, mp)
    other = (sec, seq + 1 - 2 * core, mp)
    along = {d: (sec, lax.rem(seq + 4 * d, 16), mp) for d in (1, 2, 3)}
    return across, other, along


class SeqGather:
    def __init__(self, copies, buf, sec, seq, mp):
        self.copies = copies
        self.buf = buf
        self.seq = seq
        self.across, self.other, self.along = seq_peers(sec, seq, mp)
        self.z_slot = copies.slot()
        self.y_slot = {(t, d): copies.slot() for t in (0, 1) for d in (1, 2, 3)}
        self.c_slot = {(t, d): copies.slot() for t in (0, 1) for d in (0, 1, 2, 3)}

    def index(self, t, d):
        own = lax.rem(self.seq + 16 - 4 * d, 16)
        if t == 0:
            return own
        return own + 2 - 4 * lax.rem(own // 2, 2)

    def send(self, slot, t, d, device):
        block = self.buf.at[self.index(t, d)]
        self.copies.start(slot, block, block, device)

    def begin_far(self):
        self.send(self.z_slot, 0, 0, self.across)

    def begin_near(self):
        for d in (1, 3, 2):
            self.send(self.y_slot[0, d], 0, 0, self.along[d])
        self.send(self.c_slot[0, 0], 0, 0, self.other)

    def relay_across(self):
        self.copies.wait_recv(self.z_slot, self.buf.at[0], self.across)
        for d in (1, 3, 2):
            self.send(self.y_slot[1, d], 1, 0, self.along[d])
        self.send(self.c_slot[1, 0], 1, 0, self.other)

    def relay_core(self, t, d):
        self.copies.wait_recv(self.y_slot[t, d], self.buf.at[0], self.along[d])
        self.send(self.c_slot[t, d], t, d, self.other)

    def end(self):
        for t in (0, 1):
            for d in (0, 1, 2, 3):
                self.copies.wait_recv(self.c_slot[t, d], self.buf.at[0], self.other)


def layer_kernel(
    order,
    q_ref,
    g_ref,
    rows_ref,
    weight_ref,
    att_ref,
    dq_ref,
    out_ref,
    rows_all,
    weight_all,
    kv_all,
    q_all,
    g_all,
    kv_t,
    score,
    prob,
    dscore,
    dquery,
    stats,
    rows_t,
    acc,
    keep,
    core_out,
    core_in,
    y_out,
    y_in,
    z_out,
    z_in,
    grad,
    send_sem,
    recv_sem,
):
    sec, seq, mp = place()
    copies = Copies(send_sem, recv_sem)
    yy = seq // 4
    core = lax.rem(seq, 2)
    across, other, along = seq_peers(sec, seq, mp)
    sec_peer = {d: (lax.rem(sec + d, 4), seq, mp) for d in (1, 2, 3)}
    mp_peer = {d: (sec, seq, lax.rem(mp + d, 4)) for d in (1, 2, 3)}
    own = sec * 4 + mp
    diagonal = seq == own
    mirror = (seq // 4, own, lax.rem(seq, 4))

    barrier = pltpu.get_barrier_semaphore()
    peers = (
        [mp_peer[d] for d in (1, 2, 3)]
        + [sec_peer[d] for d in (1, 2, 3)]
        + [along[d] for d in (1, 2, 3)]
        + [across, other]
    )
    for peer in peers:
        pl.semaphore_signal(barrier, inc=1, device_id=peer, device_id_type=MESH)

    @pl.when(jnp.logical_not(diagonal))
    def _():
        pl.semaphore_signal(barrier, inc=1, device_id=mirror, device_id_type=MESH)

    rows_all[own] = rows_ref[...]
    weight_all[seq] = weight_ref[0]
    pl.semaphore_wait(barrier, len(peers) + 1 - diagonal.astype(jnp.int32))

    gather_w = SeqGather(copies, weight_all, sec, seq, mp)
    gather_kv = SeqGather(copies, kv_all, sec, seq, mp)
    rows_slot = {d: copies.slot() for d in (1, 2, 3)}
    along_x = {(e, d): copies.slot() for e in range(4) for d in (1, 2, 3)}
    turn_slot = copies.slot()
    m_slot = {d: copies.slot() for d in (1, 2, 3)}
    x_slot = {(e, d): copies.slot() for e in range(4) for d in (1, 2, 3)}
    core_slot = [copies.slot() for _ in range(4)]
    y_slot = {d: copies.slot() for d in (1, 2, 3)}
    z_slot = [copies.slot() for _ in range(PIECES)]
    ag_slot = {(p, d): copies.slot() for p in range(PIECES) for d in (1, 2, 3)}
    cg_slot = {(p, d): copies.slot() for p in range(PIECES) for d in (0, 1, 2, 3)}

    tok = q_ref.shape[0]
    half = tok // SLOTS
    group = q_ref.shape[1] // HD
    lanes = group * half
    part_rows = 4 * tok
    scale = HD ** (-0.5)
    rate = scale * LOG2E

    def token_block(t):
        return rows_t.at[t // 2, pl.ds(pl.multiple_of(lax.rem(t, 2) * tok, 16), tok), :]

    def pass_on(e):
        block = token_block(sec * 4 + lax.rem(mp + 4 - e, 4))
        if e:
            copies.wait_recv(m_slot[e], block, mp_peer[e])
        for d in (1, 3, 2):
            copies.start(x_slot[e, d], block, block, sec_peer[d])

    def lane(i):
        return slice(i * lanes, (i + 1) * lanes)

    def pass_rows(e):
        block = rows_all.at[sec * 4 + lax.rem(mp + 4 - e, 4)]
        if e:
            copies.wait_recv(rows_slot[e], block, mp_peer[e])
        for d in (1, 3, 2):
            copies.start(along_x[e, d], block, block, sec_peer[d])

    block = rows_all.at[own]
    for d in (1, 3):
        copies.start(rows_slot[d], block, block, mp_peer[d])
    pass_rows(0)
    gather_w.begin_near()
    for i in range(SLOTS):
        for h in range(group):
            at = i * lanes + h * half
            rows = slice(i * half, (i + 1) * half)
            q_all[at : at + half, :] = q_ref[rows, h * HD : (h + 1) * HD]
            g_all[at : at + half, :] = g_ref[rows, h * HD : (h + 1) * HD]
    pass_rows(1)
    gather_w.begin_far()
    pass_rows(3)
    copies.start(rows_slot[2], block, block, mp_peer[2])
    for d in (1, 3, 2):
        gather_w.relay_core(0, d)
    gather_w.relay_across()
    pass_rows(2)
    for d in (1, 3, 2):
        gather_w.relay_core(1, d)
    for e in (0, 1, 3, 2):
        for d in (1, 3, 2):
            copies.wait_recv(along_x[e, d], block, sec_peer[d])

    turn = copies.make(turn_slot, block, token_block(seq), mirror)

    @pl.when(diagonal)
    def _():
        token_block(own)[...] = rows_ref[...]

    @pl.when(jnp.logical_not(diagonal))
    def _():
        turn.start()

    gather_w.end()

    def term(f, total):
        return total + jnp.dot(
            rows_all[f], weight_all[f], preferred_element_type=jnp.float32
        )

    total = lax.fori_loop(0, 16, term, jnp.zeros((tok, 2 * HD), jnp.float32))
    kv_all[seq] = total.astype(jnp.bfloat16)

    gather_kv.begin_far()
    gather_kv.begin_near()

    def keys_of(d):
        first = lax.rem(yy + 4 - d, 4) * 4
        return kv_all[pl.ds(first, 4)].reshape(part_rows, 2 * HD)

    skew = lax.broadcasted_iota(jnp.int32, (half, lanes), 0) - lax.rem(
        lax.broadcasted_iota(jnp.int32, (half, lanes), 1), half
    )
    peaks = [jnp.full((8, lanes), -1e30, jnp.float32) for _ in range(SLOTS)]

    def look(d):
        for t in (0, 1):
            copies.wait_recv(gather_kv.c_slot[t, d], kv_all.at[0], other)
        part_kv = keys_of(d)
        kv_t[d] = part_kv.T
        first = lax.rem(yy + 4 - d, 4) * (part_rows // half)
        for i in range(SLOTS):
            raw = contract(part_kv[:, :HD], q_all[lane(i), :], 1, 1)
            for b in range(part_rows // half):
                ahead = (order[seq * SLOTS + i] - order[first + b]) * half
                seen = jnp.where(skew <= ahead, raw[b * half : (b + 1) * half, :], -1e30)
                at = d * part_rows + b * half
                score[at : at + half, lane(i)] = seen
                peaks[i] = jnp.maximum(
                    peaks[i], jnp.max(seen.reshape(half // 8, 8, lanes), axis=0)
                )

    for d in (1, 3, 2):
        gather_kv.relay_core(0, d)
    gather_kv.relay_across()

    def pass_on(e):
        block = token_block(sec * 4 + lax.rem(mp + 4 - e, 4))
        if e:
            copies.wait_recv(m_slot[e], block, mp_peer[e])
        for d in (1, 3, 2):
            copies.start(x_slot[e, d], block, block, sec_peer[d])

    look(0)
    for d in (1, 3, 2):
        gather_kv.relay_core(1, d)

    @pl.when(jnp.logical_not(diagonal))
    def _():
        turn.wait_send()
        copies.wait_recv(turn_slot, token_block(own), mirror)

    for d in (1, 3, 2):
        copies.start(m_slot[d], token_block(own), token_block(own), mp_peer[d])
    pass_on(0)
    look(1)
    look(3)
    look(2)
    for i in range(SLOTS):
        peak = jnp.max(peaks[i], axis=0, keepdims=True)
        total = jnp.zeros((8, lanes), jnp.float32)
        for d in range(4):
            at = slice(d * part_rows, (d + 1) * part_rows)
            expo = jnp.exp2((score[at, lane(i)] - peak) * rate)
            score[at, lane(i)] = expo
            total += jnp.sum(expo.reshape(part_rows // 8, 8, lanes), axis=0)
        part = 1.0 / jnp.sum(total, axis=0, keepdims=True)
        out = jnp.zeros((HD, lanes), jnp.float32)
        for d in range(4):
            at = slice(d * part_rows, (d + 1) * part_rows)
            weights = (score[at, lane(i)] * part).astype(jnp.bfloat16)
            prob[at, lane(i)] = weights
            out += jnp.dot(kv_t[d, HD:], weights, preferred_element_type=jnp.float32)
        out = out.astype(jnp.bfloat16).astype(jnp.float32)
        delta = jnp.sum(g_all[lane(i), :].astype(jnp.float32).T * out, axis=0, keepdims=True)
        stats[0, :, lane(i)] = jnp.broadcast_to(delta, (8, lanes))
        stats[1, :, lane(i)] = jnp.broadcast_to(part * scale, (8, lanes))
        out = out.T.astype(jnp.bfloat16)
        for h in range(group):
            att_ref[i * half : (i + 1) * half, h * HD : (h + 1) * HD] = out[
                h * half : (h + 1) * half, :
            ]
        if i == 0:
            pass_on(1)
        if i == 1:
            pass_on(3)
        if i == 3:
            pass_on(2)

    def back(d):
        part = (4 - d) % 4
        rows = slice(part * part_rows, (part + 1) * part_rows)
        values = keys_of(part)[:, HD:]
        for i in range(SLOTS):
            dprob = contract(values, g_all[lane(i), :], 1, 1)
            dscore[:, lane(i)] = (
                score[rows, lane(i)]
                * stats[1, :1, lane(i)]
                * (dprob - stats[0, :1, lane(i)])
            ).astype(jnp.bfloat16)
        dkey = jnp.dot(dscore[...], q_all[...], preferred_element_type=jnp.float32)
        dvalue = jnp.dot(prob[rows, :], g_all[...], preferred_element_type=jnp.float32)
        acc[..., :HD] = dkey.reshape(2, 2, tok, HD)
        acc[..., HD:] = dvalue.reshape(2, 2, tok, HD)
        core_out[d] = acc[:, 1 - core].astype(jnp.bfloat16)
        copies.start(core_slot[d], core_out.at[d], core_in.at[d], other)
        keep[d] = acc[:, core]
        more = jnp.dot(kv_t[part, :HD], dscore[...], preferred_element_type=jnp.float32)
        if d == 2:
            dquery[...] = more
        else:
            dquery[...] += more

    def send_along(d):
        copies.wait_recv(core_slot[d], core_in.at[d], other)
        y_out[d - 1] = (keep[d] + core_in[d].astype(jnp.float32)).astype(jnp.bfloat16)
        copies.start(y_slot[d], y_out.at[d - 1], y_in.at[d - 1], along[d])

    back(2)
    back(1)
    send_along(2)
    back(3)
    send_along(1)
    back(0)
    send_along(3)
    for i in range(SLOTS):
        turned = dquery[:, lane(i)].T.astype(jnp.bfloat16)
        for h in range(group):
            dq_ref[i * half : (i + 1) * half, h * HD : (h + 1) * HD] = turned[
                h * half : (h + 1) * half, :
            ]
    copies.wait_recv(core_slot[0], core_in.at[0], other)
    for d in (1, 3, 2):
        copies.wait_recv(y_slot[d], y_in.at[d - 1], along[d])

    piece = tok // PIECES

    def piece_rows(p):
        return slice(p * piece, (p + 1) * piece)

    for p in range(PIECES):
        rows = piece_rows(p)
        total = keep[0, :, rows] + core_in[0, :, rows].astype(jnp.float32)
        for d in (1, 2, 3):
            total += y_in[d - 1, :, rows].astype(jnp.float32)
        z_out[p] = total.astype(jnp.bfloat16)
        copies.start(z_slot[p], z_out.at[p], z_in.at[p], across)
    for p in range(PIECES):
        copies.wait_recv(z_slot[p], z_in.at[p], across)
        grad[yy, :, core, piece_rows(p)] = (
            z_out[p].astype(jnp.float32) + z_in[p].astype(jnp.float32)
        ).astype(jnp.bfloat16)
        mine = grad.at[yy, :, core, piece_rows(p)]
        for d in (1, 3, 2):
            copies.start(ag_slot[p, d], mine, mine, along[d])
        copies.start(cg_slot[p, 0], mine, mine, other)
    for p in range(PIECES):
        for d in (1, 3, 2):
            block = grad.at[lax.rem(yy + 4 - d, 4), :, core, piece_rows(p)]
            copies.wait_recv(ag_slot[p, d], block, along[d])
            copies.start(cg_slot[p, d], block, block, other)
    for j in range(4):
        for d in (1, 3, 2):
            copies.wait_recv(x_slot[j, d], token_block(own), sec_peer[d])
    for p in range(PIECES):
        for d in (0, 1, 3, 2):
            copies.wait_recv(cg_slot[p, d], grad.at[0, :, 0, piece_rows(p)], other)

    result = jnp.zeros(out_ref.shape, jnp.float32)
    for k in range(8):
        block = grad[k // 2, k % 2].reshape(2 * tok, 2 * HD)
        result += contract(rows_t[k], block, 0, 0)
    out_ref[...] = result

    copies.finish()


def layer(order, queries, out_grad, rows, weight):
    tok, cols = queries.shape
    feat = rows.shape[1]
    keys = 16 * tok
    lanes = cols // HD * tok
    sems = 15 + 15 + 15 + 1 + 15 + 4 + 3 + PIECES * 8
    vmem = pl.BlockSpec(memory_space=pltpu.VMEM)
    half = (2, tok, 2 * HD)
    pieces = (PIECES, 2, tok // PIECES, 2 * HD)
    return pl.pallas_call(
        layer_kernel,
        out_shape=(
            jax.ShapeDtypeStruct((tok, cols), jnp.bfloat16),
            jax.ShapeDtypeStruct((tok, cols), jnp.bfloat16),
            jax.ShapeDtypeStruct((feat, 2 * HD), jnp.float32),
        ),
        in_specs=[pl.BlockSpec(memory_space=pltpu.SMEM)] + [vmem] * 4,
        out_specs=(vmem, vmem, vmem),
        scratch_shapes=[
            pltpu.VMEM((16, tok, feat), jnp.bfloat16),
            pltpu.VMEM((16, feat, 2 * HD), jnp.bfloat16),
            pltpu.VMEM((16, tok, 2 * HD), jnp.bfloat16),
            pltpu.VMEM((lanes, HD), jnp.bfloat16),
            pltpu.VMEM((lanes, HD), jnp.bfloat16),
            pltpu.VMEM((4, 2 * HD, keys // 4), jnp.bfloat16),
            pltpu.VMEM((keys, lanes), jnp.float32),
            pltpu.VMEM((keys, lanes), jnp.bfloat16),
            pltpu.VMEM((keys // 4, lanes), jnp.bfloat16),
            pltpu.VMEM((HD, lanes), jnp.float32),
            pltpu.VMEM((2, 8, lanes), jnp.float32),
            pltpu.VMEM((8, 2 * tok, feat), jnp.bfloat16),
            pltpu.VMEM((2,) + half, jnp.float32),
            pltpu.VMEM((4,) + half, jnp.float32),
            pltpu.VMEM((4,) + half, jnp.bfloat16),
            pltpu.VMEM((4,) + half, jnp.bfloat16),
            pltpu.VMEM((3,) + half, jnp.bfloat16),
            pltpu.VMEM((3,) + half, jnp.bfloat16),
            pltpu.VMEM(pieces, jnp.bfloat16),
            pltpu.VMEM(pieces, jnp.bfloat16),
            pltpu.VMEM((4, 2) + half, jnp.bfloat16),
            pltpu.SemaphoreType.DMA((sems,)),
            pltpu.SemaphoreType.DMA((sems,)),
        ],
        compiler_params=pltpu.CompilerParams(
            collective_id=0, has_side_effects=True, vmem_limit_bytes=VMEM_LIMIT
        ),
        name="layer",
    )(order, queries, out_grad, rows, weight)


def body(rows40, queries, kv_weight, out_grad, block_order):
    attended, query_grad, grad = layer(block_order, queries[0], out_grad[0], rows40, kv_weight)
    return (attended[None], query_grad[None], grad[None])


def solution(mesh):
    return jax.shard_map(
        body,
        mesh=mesh,
        in_specs=(
            P("seq", ("section", "mp")),
            P("section", "seq", "mp"),
            P("section", "seq", "mp"),
            P("section", "seq", "mp"),
            P(),
        ),
        out_specs=(P("section", "seq", "mp"), P("section", "seq", "mp"), P("section", "seq", "mp")),
        check_vma=False,
    )
```

```python
import functools

import jax
import jax.numpy as jnp
from jax import lax
import jax.experimental.pallas as pl
import jax.experimental.pallas.tpu as pltpu
from jax.sharding import PartitionSpec as P

HD = 128
SLOTS = 4
PIECES = 4
VMEM_LIMIT = 60 * 2**20
MESH = pl.DeviceIdType.MESH
LOG2E = 1.4426950408889634


def contract(left, right, left_dim, right_dim):
    return lax.dot_general(
        left,
        right,
        (((left_dim,), (right_dim,)), ((), ())),
        preferred_element_type=jnp.float32,
    )


class Copies:
    def __init__(self, send_sem, recv_sem):
        self.send_sem = send_sem
        self.recv_sem = recv_sem
        self.count = 0
        self.started = []
        self.guarded = []

    def slot(self):
        self.count += 1
        return self.count - 1

    def make(self, slot, src, dst, device):
        return pltpu.make_async_remote_copy(
            src_ref=src,
            dst_ref=dst,
            send_sem=self.send_sem.at[slot],
            recv_sem=self.recv_sem.at[slot],
            device_id=device,
            device_id_type=MESH,
        )

    def start(self, slot, src, dst, device):
        copy = self.make(slot, src, dst, device)
        copy.start()
        self.started.append(copy)

    def wait_recv(self, slot, buf, device):
        self.make(slot, buf, buf, device).wait_recv()

    def start_if(self, slot, ref, device, condition):
        @pl.when(condition())
        def _():
            self.make(slot, ref(), ref(), device).start()

        self.guarded.append((slot, ref, device, condition))

    def finish(self):
        for copy in self.started:
            copy.wait_send()
        for slot, ref, device, condition in self.guarded:

            @pl.when(condition())
            def _():
                self.make(slot, ref(), ref(), device).wait_send()


def place():
    sec = lax.axis_index("section")
    seq = lax.axis_index("seq")
    mp = lax.axis_index("mp")
    return sec, seq, mp


def greet(peers):
    barrier = pltpu.get_barrier_semaphore()
    for peer in peers:
        pl.semaphore_signal(barrier, inc=1, device_id=peer, device_id_type=MESH)
    pl.semaphore_wait(barrier, len(peers))


def seq_peers(sec, seq, mp):
    zhi = lax.rem(seq // 2, 2)
    core = lax.rem(seq, 2)
    across = (sec, seq + 2 - 4 * zhi, mp)
    other = (sec, seq + 1 - 2 * core, mp)
    along = {d: (sec, lax.rem(seq + 4 * d, 16), mp) for d in (1, 2, 3)}
    return across, other, along


class SeqGather:
    def __init__(self, copies, buf, rows, sec, seq, mp):
        self.copies = copies
        self.buf = buf
        self.rows = rows
        self.seq = seq
        self.across, self.other, self.along = seq_peers(sec, seq, mp)
        self.z_slot = copies.slot()
        self.y_slot = {(t, d): copies.slot() for t in (0, 1) for d in (1, 2, 3)}
        self.c_slot = {(t, d): copies.slot() for t in (0, 1) for d in (0, 1, 2, 3)}

    def block(self, t, d):
        owner = lax.rem(self.seq + 16 - 4 * d, 16)
        if t:
            owner = owner + 2 - 4 * lax.rem(owner // 2, 2)
        return self.buf.at[owner, self.rows]

    def send(self, slot, t, d, device):
        block = self.block(t, d)
        self.copies.start(slot, block, block, device)

    def begin_far(self):
        self.send(self.z_slot, 0, 0, self.across)

    def begin_near(self, t=0):
        for d in (1, 3, 2):
            self.send(self.y_slot[t, d], t, 0, self.along[d])
        self.send(self.c_slot[t, 0], t, 0, self.other)

    def relay_across(self):
        self.copies.wait_recv(self.z_slot, self.block(1, 0), self.across)
        self.begin_near(1)

    def relay_core(self, t):
        for d in (1, 3, 2):
            self.copies.wait_recv(self.y_slot[t, d], self.block(t, d), self.along[d])
            self.send(self.c_slot[t, d], t, d, self.other)

    def end(self, d):
        for t in (0, 1):
            self.copies.wait_recv(self.c_slot[t, d], self.block(t, d), self.other)


def layer_kernel(
    order,
    q_ref,
    g_ref,
    rows_ref,
    weight_ref,
    att_ref,
    dq_ref,
    out_ref,
    rows_all,
    weight_all,
    kv_all,
    q_all,
    g_all,
    kv_t,
    score,
    prob,
    dscore,
    dquery,
    stats,
    rows_t,
    rows_tt,
    acc,
    keep,
    core_out,
    core_in,
    y_out,
    y_in,
    z_out,
    z_in,
    grad,
    send_sem,
    recv_sem,
):
    sec, seq, mp = place()
    copies = Copies(send_sem, recv_sem)
    yy = seq // 4
    core = lax.rem(seq, 2)
    across, other, along = seq_peers(sec, seq, mp)
    sec_peer = {d: (lax.rem(sec + d, 4), seq, mp) for d in (1, 2, 3)}
    mp_peer = {d: (sec, seq, lax.rem(mp + d, 4)) for d in (1, 2, 3)}
    own = sec * 4 + mp
    zhi = lax.rem(seq // 2, 2)
    turning = mp // 2 != zhi
    mirror = (seq // 4, own, lax.rem(seq, 4))
    aslant = {d: (sec, lax.rem(seq + 4 * d, 16) + 1 - 2 * core, mp) for d in (1, 2, 3)}

    barrier = pltpu.get_barrier_semaphore()
    peers = (
        [mp_peer[d] for d in (1, 2, 3)]
        + [sec_peer[d] for d in (1, 2, 3)]
        + [along[d] for d in (1, 2, 3)]
        + [aslant[d] for d in (1, 2, 3)]
        + [across, other]
    )
    for peer in peers:
        pl.semaphore_signal(barrier, inc=1, device_id=peer, device_id_type=MESH)

    @pl.when(turning)
    def _():
        pl.semaphore_signal(barrier, inc=1, device_id=mirror, device_id_type=MESH)

    rows_all[own] = rows_ref[...]
    weight_all[seq] = weight_ref[0]
    pl.semaphore_wait(barrier, len(peers) + turning.astype(jnp.int32))

    w_rows, kv_rows = weight_all.shape[1] // 2, kv_all.shape[1] // 2
    gather_w = [
        SeqGather(copies, weight_all, pl.ds(p * w_rows, w_rows), sec, seq, mp) for p in (0, 1)
    ]
    gather_kv = [
        SeqGather(copies, kv_all, pl.ds(p * kv_rows, kv_rows), sec, seq, mp) for p in (0, 1)
    ]
    sides = [(side, hops) for hops in (1, 2, 3) for side in (-1, 1)]
    line_slot = {key: copies.slot() for key in sides}
    along_x = {(key, d): copies.slot() for key in [(0, 0)] + sides for d in (1, 2, 3)}
    turn_slot = copies.slot()
    m_slot = {(j, d): copies.slot() for j in (0, 1) for d in (1, 2, 3)}
    x_slot = {(j, d): copies.slot() for j in (0, 1) for d in (1, 2, 3)}
    y_same = {d: copies.slot() for d in (1, 2, 3)}
    y_cross = {d: copies.slot() for d in (0, 1, 2, 3)}
    core_slot = [copies.slot() for _ in range(4)]
    y_slot = {d: copies.slot() for d in (1, 2, 3)}
    z_slot = [copies.slot() for _ in range(PIECES)]
    ag_slot = {(p, d): copies.slot() for p in range(PIECES) for d in (1, 2, 3)}
    cg_slot = {(p, d): copies.slot() for p in range(PIECES) for d in (0, 1, 2, 3)}

    tok = q_ref.shape[0]
    half = tok // SLOTS
    group = q_ref.shape[1] // HD
    lanes = group * half
    part_rows = 4 * tok
    scale = HD ** (-0.5)
    rate = scale * LOG2E

    def token_block(t):
        return rows_t.at[t // 2, pl.ds(pl.multiple_of(lax.rem(t, 2) * tok, 16), tok), :]

    def pass_on(e):
        block = token_block(sec * 4 + lax.rem(mp + 4 - e, 4))
        if e:
            copies.wait_recv(m_slot[e], block, mp_peer[e])
        for d in (1, 3, 2):
            copies.start(x_slot[e, d], block, block, sec_peer[d])

    def lane(i):
        return slice(i * lanes, (i + 1) * lanes)

    below = (sec, seq, jnp.maximum(mp - 1, 0))
    above = (sec, seq, jnp.minimum(mp + 1, 3))

    def there(key):
        side, hops = key
        return mp >= hops if side < 0 else mp + hops <= 3

    def rows_of(key):
        side, hops = key
        return rows_all.at[sec * 4 + mp + side * hops]

    def spread(key):
        for d in (1, 3, 2):
            copies.start_if(
                along_x[key, d],
                lambda: rows_of(key),
                sec_peer[d],
                lambda: there(key),
            )

    def from_line(hops):
        for side in (-1, 1):
            key = (side, hops)

            @pl.when(there(key))
            def _():
                copies.wait_recv(line_slot[key], rows_of(key), below if side < 0 else above)

            if hops < 3:
                to_line(key)
            spread(key)

    def to_line(key):
        side, hops = key
        copies.start_if(
            line_slot[side, hops + 1],
            lambda: rows_of(key),
            above if side < 0 else below,
            lambda: jnp.logical_and(there(key), mp < 3 if side < 0 else mp > 0),
        )

    to_line((-1, 0))
    to_line((1, 0))
    spread((0, 0))
    gather_w[0].begin_far()
    gather_w[0].begin_near()
    gather_w[1].begin_near()
    for i in range(SLOTS):
        for h in range(group):
            at = i * lanes + h * half
            rows = slice(i * half, (i + 1) * half)
            q_all[at : at + half, :] = q_ref[rows, h * HD : (h + 1) * HD]
            g_all[at : at + half, :] = g_ref[rows, h * HD : (h + 1) * HD]
    from_line(1)
    gather_w[1].begin_far()
    gather_w[0].relay_across()
    from_line(2)
    gather_w[0].relay_core(0)
    gather_w[1].relay_core(0)
    gather_w[1].relay_across()
    turn = copies.make(turn_slot, rows_all.at[own], token_block(seq), mirror)

    @pl.when(turning)
    def _():
        turn.start()

    from_line(3)
    gather_w[0].relay_core(1)
    gather_w[1].relay_core(1)

    for key in [(0, 0)] + sides:

        @pl.when(there(key))
        def _():
            for d in (1, 3, 2):
                copies.wait_recv(along_x[key, d], rows_of(key), sec_peer[d])

    for p in (0, 1):
        for d in range(4):
            gather_w[p].end(d)

    total = jnp.zeros((tok, 2 * HD), jnp.float32)
    for f in range(16):
        total += jnp.dot(rows_all[f], weight_all[f], preferred_element_type=jnp.float32)
    kv_all[seq] = total.astype(jnp.bfloat16)

    for p in (0, 1):
        gather_kv[p].begin_far()
    for p in (0, 1):
        gather_kv[p].begin_near()

    def keys_of(d):
        first = lax.rem(yy + 4 - d, 4) * 4
        return kv_all[pl.ds(first, 4)].reshape(part_rows, 2 * HD)

    skew = lax.broadcasted_iota(jnp.int32, (half, lanes), 0) - lax.rem(
        lax.broadcasted_iota(jnp.int32, (half, lanes), 1), half
    )
    peaks = [jnp.full((8, lanes), -1e30, jnp.float32) for _ in range(SLOTS)]

    def look(d):
        for p in (0, 1):
            gather_kv[p].end(d)
        part_kv = keys_of(d)
        kv_t[d] = part_kv.T
        first = lax.rem(yy + 4 - d, 4) * (part_rows // half)
        for i in range(SLOTS):
            raw = contract(part_kv[:, :HD], q_all[lane(i), :], 1, 1)
            for b in range(part_rows // half):
                ahead = (order[seq * SLOTS + i] - order[first + b]) * half
                seen = jnp.where(skew <= ahead, raw[b * half : (b + 1) * half, :], -1e30)
                at = d * part_rows + b * half
                score[at : at + half, lane(i)] = seen
                peaks[i] = jnp.maximum(
                    peaks[i], jnp.max(seen.reshape(half // 8, 8, lanes), axis=0)
                )

    first_far = 2 - 2 * zhi

    def far_block(j):
        return token_block(sec * 4 + first_far + j)

    def has_far(j):
        return jnp.logical_and(turning, lax.rem(mp, 2) == j)

    def begin_line():
        @pl.when(turning)
        def _():
            turn.wait_send()
            copies.wait_recv(turn_slot, token_block(own), mirror)

        for j in (0, 1):
            for d in (1, 3, 2):
                copies.start_if(
                    m_slot[j, d], lambda j=j: far_block(j), mp_peer[d], lambda j=j: has_far(j)
                )

    def pass_on(j):
        for d in (1, 2, 3):
            @pl.when(first_far + j == lax.rem(mp + 4 - d, 4))
            def _():
                copies.wait_recv(m_slot[j, d], far_block(j), mp_peer[d])

        for d in (1, 3, 2):
            copies.start(x_slot[j, d], far_block(j), far_block(j), sec_peer[d])

    def along_y():
        token_block(seq)[...] = rows_all[seq]
        for d in (1, 3, 2):
            aim = lax.rem(seq + 4 * d, 16)
            copies.start(y_same[d], rows_all.at[aim], token_block(seq), along[d])
            aim = aim + 1 - 2 * core
            copies.start(y_cross[d], rows_all.at[aim], token_block(seq), aslant[d])
        copies.start(y_cross[0], rows_all.at[seq + 1 - 2 * core], token_block(seq), other)

    def end_blocks():
        for d in (1, 3, 2):
            copies.wait_recv(y_same[d], token_block(seq), along[d])
            copies.wait_recv(y_cross[d], token_block(seq), aslant[d])
        copies.wait_recv(y_cross[0], token_block(seq), other)
        for j in (0, 1):
            for d in (1, 3, 2):
                copies.wait_recv(x_slot[j, d], far_block(j), sec_peer[d])

    gather_kv[0].relay_core(0)
    gather_kv[0].relay_across()
    gather_kv[1].relay_core(0)
    gather_kv[1].relay_across()

    begin_line()
    look(0)
    gather_kv[0].relay_core(1)
    gather_kv[1].relay_core(1)
    along_y()
    look(1)
    look(3)
    look(2)
    for i in range(SLOTS):
        peak = jnp.max(peaks[i], axis=0, keepdims=True)
        total = jnp.zeros((8, lanes), jnp.float32)
        for d in range(4):
            at = slice(d * part_rows, (d + 1) * part_rows)
            expo = jnp.exp2((score[at, lane(i)] - peak) * rate)
            score[at, lane(i)] = expo
            total += jnp.sum(expo.reshape(part_rows // 8, 8, lanes), axis=0)
        part = 1.0 / jnp.sum(total, axis=0, keepdims=True)
        out = jnp.zeros((HD, lanes), jnp.float32)
        for d in range(4):
            at = slice(d * part_rows, (d + 1) * part_rows)
            weights = (score[at, lane(i)] * part).astype(jnp.bfloat16)
            prob[at, lane(i)] = weights
            out += jnp.dot(kv_t[d, HD:], weights, preferred_element_type=jnp.float32)
        out = out.astype(jnp.bfloat16).astype(jnp.float32)
        delta = jnp.sum(g_all[lane(i), :].astype(jnp.float32).T * out, axis=0, keepdims=True)
        stats[0, :, lane(i)] = jnp.broadcast_to(delta, (8, lanes))
        stats[1, :, lane(i)] = jnp.broadcast_to(part * scale, (8, lanes))
        out = out.T.astype(jnp.bfloat16)
        for h in range(group):
            att_ref[i * half : (i + 1) * half, h * HD : (h + 1) * HD] = out[
                h * half : (h + 1) * half, :
            ]
        if i < 2:
            pass_on(i)

    def back(d, between=None):
        part = (4 - d) % 4
        rows = slice(part * part_rows, (part + 1) * part_rows)
        values = keys_of(part)[:, HD:]
        for i in range(SLOTS):
            dprob = contract(values, g_all[lane(i), :], 1, 1)
            dscore[:, lane(i)] = (
                score[rows, lane(i)]
                * stats[1, :1, lane(i)]
                * (dprob - stats[0, :1, lane(i)])
            ).astype(jnp.bfloat16)
        if between:
            send_along(between)
        dkey = jnp.dot(dscore[...], q_all[...], preferred_element_type=jnp.float32)
        dvalue = jnp.dot(prob[rows, :], g_all[...], preferred_element_type=jnp.float32)
        acc[..., :HD] = dkey.reshape(2, 2, tok, HD)
        acc[..., HD:] = dvalue.reshape(2, 2, tok, HD)
        core_out[d] = acc[:, 1 - core].astype(jnp.bfloat16)
        copies.start(core_slot[d], core_out.at[d], core_in.at[d], other)
        keep[d] = acc[:, core]
        more = jnp.dot(kv_t[part, :HD], dscore[...], preferred_element_type=jnp.float32)
        if d == 2:
            dquery[...] = more
        else:
            dquery[...] += more

    def send_along(d):
        copies.wait_recv(core_slot[d], core_in.at[d], other)
        y_out[d - 1] = (keep[d] + core_in[d].astype(jnp.float32)).astype(jnp.bfloat16)
        copies.start(y_slot[d], y_out.at[d - 1], y_in.at[d - 1], along[d])

    back(2)
    back(1, between=2)
    back(3, between=1)
    back(0, between=3)
    for i in range(SLOTS):
        turned = dquery[:, lane(i)].T.astype(jnp.bfloat16)
        for h in range(group):
            dq_ref[i * half : (i + 1) * half, h * HD : (h + 1) * HD] = turned[
                h * half : (h + 1) * half, :
            ]
    copies.wait_recv(core_slot[0], core_in.at[0], other)
    for d in (1, 3, 2):
        copies.wait_recv(y_slot[d], y_in.at[d - 1], along[d])

    piece = tok // PIECES

    def piece_rows(p):
        return slice(p * piece, (p + 1) * piece)

    for p in range(PIECES):
        rows = piece_rows(p)
        total = keep[0, :, rows] + core_in[0, :, rows].astype(jnp.float32)
        for d in (1, 2, 3):
            total += y_in[d - 1, :, rows].astype(jnp.float32)
        z_out[p] = total.astype(jnp.bfloat16)
        copies.start(z_slot[p], z_out.at[p], z_in.at[p], across)
    end_blocks()
    for k in range(8):
        rows_tt[k] = rows_t[k].T
    for p in range(PIECES):
        copies.wait_recv(z_slot[p], z_in.at[p], across)
        grad[yy, :, core, piece_rows(p)] = (
            z_out[p].astype(jnp.float32) + z_in[p].astype(jnp.float32)
        ).astype(jnp.bfloat16)
        mine = grad.at[yy, :, core, piece_rows(p)]
        for d in (1, 3, 2):
            copies.start(ag_slot[p, d], mine, mine, along[d])
        copies.start(cg_slot[p, 0], mine, mine, other)
    for p in range(PIECES):
        for d in (1, 3, 2):
            block = grad.at[lax.rem(yy + 4 - d, 4), :, core, piece_rows(p)]
            copies.wait_recv(ag_slot[p, d], block, along[d])
            copies.start(cg_slot[p, d], block, block, other)
    for d in (0, 1, 3, 2):
        for p in range(PIECES):
            copies.wait_recv(cg_slot[p, d], grad.at[0, :, 0, piece_rows(p)], other)
        yt = lax.rem(yy + 4 - d, 4)
        more = sum(
            jnp.dot(
                rows_tt[2 * yt + t],
                grad[yt, t].reshape(2 * tok, 2 * HD),
                preferred_element_type=jnp.float32,
            )
            for t in (0, 1)
        )
        if d == 0:
            out_ref[...] = more
        else:
            out_ref[...] += more

    copies.finish()


def layer(order, queries, out_grad, rows, weight):
    tok, cols = queries.shape
    feat = rows.shape[1]
    keys = 16 * tok
    lanes = cols // HD * tok
    sems = 4 * 15 + 6 + 21 + 1 + 19 + 4 + 3 + PIECES * 8
    vmem = pl.BlockSpec(memory_space=pltpu.VMEM)
    half = (2, tok, 2 * HD)
    pieces = (PIECES, 2, tok // PIECES, 2 * HD)
    return pl.pallas_call(
        layer_kernel,
        out_shape=(
            jax.ShapeDtypeStruct((tok, cols), jnp.bfloat16),
            jax.ShapeDtypeStruct((tok, cols), jnp.bfloat16),
            jax.ShapeDtypeStruct((feat, 2 * HD), jnp.float32),
        ),
        in_specs=[pl.BlockSpec(memory_space=pltpu.SMEM)] + [vmem] * 4,
        out_specs=(vmem, vmem, vmem),
        scratch_shapes=[
            pltpu.VMEM((16, tok, feat), jnp.bfloat16),
            pltpu.VMEM((16, feat, 2 * HD), jnp.bfloat16),
            pltpu.VMEM((16, tok, 2 * HD), jnp.bfloat16),
            pltpu.VMEM((lanes, HD), jnp.bfloat16),
            pltpu.VMEM((lanes, HD), jnp.bfloat16),
            pltpu.VMEM((4, 2 * HD, keys // 4), jnp.bfloat16),
            pltpu.VMEM((keys, lanes), jnp.float32),
            pltpu.VMEM((keys, lanes), jnp.bfloat16),
            pltpu.VMEM((keys // 4, lanes), jnp.bfloat16),
            pltpu.VMEM((HD, lanes), jnp.float32),
            pltpu.VMEM((2, 8, lanes), jnp.float32),
            pltpu.VMEM((8, 2 * tok, feat), jnp.bfloat16),
            pltpu.VMEM((8, feat, 2 * tok), jnp.bfloat16),
            pltpu.VMEM((2,) + half, jnp.float32),
            pltpu.VMEM((4,) + half, jnp.float32),
            pltpu.VMEM((4,) + half, jnp.bfloat16),
            pltpu.VMEM((4,) + half, jnp.bfloat16),
            pltpu.VMEM((3,) + half, jnp.bfloat16),
            pltpu.VMEM((3,) + half, jnp.bfloat16),
            pltpu.VMEM(pieces, jnp.bfloat16),
            pltpu.VMEM(pieces, jnp.bfloat16),
            pltpu.VMEM((4, 2) + half, jnp.bfloat16),
            pltpu.SemaphoreType.DMA((sems,)),
            pltpu.SemaphoreType.DMA((sems,)),
        ],
        compiler_params=pltpu.CompilerParams(
            collective_id=0, has_side_effects=True, vmem_limit_bytes=VMEM_LIMIT
        ),
        name="layer",
    )(order, queries, out_grad, rows, weight)


def body(rows40, queries, kv_weight, out_grad, block_order):
    attended, query_grad, grad = layer(block_order, queries[0], out_grad[0], rows40, kv_weight)
    return (attended[None], query_grad[None], grad[None])


def solution(mesh):
    return jax.shard_map(
        body,
        mesh=mesh,
        in_specs=(
            P("seq", ("section", "mp")),
            P("section", "seq", "mp"),
            P("section", "seq", "mp"),
            P("section", "seq", "mp"),
            P(),
        ),
        out_specs=(P("section", "seq", "mp"), P("section", "seq", "mp"), P("section", "seq", "mp")),
        check_vma=False,
    )
```

```python
import functools

import jax
import jax.numpy as jnp
from jax import lax
import jax.experimental.pallas as pl
import jax.experimental.pallas.tpu as pltpu
from jax.sharding import PartitionSpec as P

HD = 128
SLOTS = 4
PIECES = 4
VMEM_LIMIT = 60 * 2**20
MESH = pl.DeviceIdType.MESH
LOG2E = 1.4426950408889634


def contract(left, right, left_dim, right_dim):
    return lax.dot_general(
        left,
        right,
        (((left_dim,), (right_dim,)), ((), ())),
        preferred_element_type=jnp.float32,
    )


class Copies:
    def __init__(self, send_sem, recv_sem):
        self.send_sem = send_sem
        self.recv_sem = recv_sem
        self.count = 0
        self.started = []
        self.guarded = []

    def slot(self):
        self.count += 1
        return self.count - 1

    def make(self, slot, src, dst, device):
        return pltpu.make_async_remote_copy(
            src_ref=src,
            dst_ref=dst,
            send_sem=self.send_sem.at[slot],
            recv_sem=self.recv_sem.at[slot],
            device_id=device,
            device_id_type=MESH,
        )

    def start(self, slot, src, dst, device):
        copy = self.make(slot, src, dst, device)
        copy.start()
        self.started.append(copy)

    def wait_recv(self, slot, buf, device):
        self.make(slot, buf, buf, device).wait_recv()

    def start_if(self, slot, ref, device, condition):
        @pl.when(condition())
        def _():
            self.make(slot, ref(), ref(), device).start()

        self.guarded.append((slot, ref, device, condition))

    def finish(self):
        for copy in self.started:
            copy.wait_send()
        for slot, ref, device, condition in self.guarded:

            @pl.when(condition())
            def _():
                self.make(slot, ref(), ref(), device).wait_send()


def place():
    sec = lax.axis_index("section")
    seq = lax.axis_index("seq")
    mp = lax.axis_index("mp")
    return sec, seq, mp


def greet(peers):
    barrier = pltpu.get_barrier_semaphore()
    for peer in peers:
        pl.semaphore_signal(barrier, inc=1, device_id=peer, device_id_type=MESH)
    pl.semaphore_wait(barrier, len(peers))


def seq_peers(sec, seq, mp):
    zhi = lax.rem(seq // 2, 2)
    core = lax.rem(seq, 2)
    across = (sec, seq + 2 - 4 * zhi, mp)
    other = (sec, seq + 1 - 2 * core, mp)
    along = {d: (sec, lax.rem(seq + 4 * d, 16), mp) for d in (1, 2, 3)}
    return across, other, along


class SeqGather:
    def __init__(self, copies, buf, rows, sec, seq, mp):
        self.copies = copies
        self.buf = buf
        self.rows = rows
        self.seq = seq
        self.across, self.other, self.along = seq_peers(sec, seq, mp)
        self.z_slot = copies.slot()
        self.y_slot = {(t, d): copies.slot() for t in (0, 1) for d in (1, 2, 3)}
        self.c_slot = {(t, d): copies.slot() for t in (0, 1) for d in (0, 1, 2, 3)}

    def block(self, t, d):
        owner = lax.rem(self.seq + 16 - 4 * d, 16)
        if t:
            owner = owner + 2 - 4 * lax.rem(owner // 2, 2)
        return self.buf.at[owner, self.rows]

    def send(self, slot, t, d, device):
        block = self.block(t, d)
        self.copies.start(slot, block, block, device)

    def begin_far(self):
        self.send(self.z_slot, 0, 0, self.across)

    def begin_near(self, t=0):
        for d in (1, 3, 2):
            self.send(self.y_slot[t, d], t, 0, self.along[d])
        self.send(self.c_slot[t, 0], t, 0, self.other)

    def relay_across(self):
        self.copies.wait_recv(self.z_slot, self.block(1, 0), self.across)
        self.begin_near(1)

    def relay_core(self, t):
        for d in (1, 3, 2):
            self.copies.wait_recv(self.y_slot[t, d], self.block(t, d), self.along[d])
            self.send(self.c_slot[t, d], t, d, self.other)

    def end(self, d, t):
        self.copies.wait_recv(self.c_slot[t, d], self.block(t, d), self.other)


def layer_kernel(
    order,
    q_ref,
    g_ref,
    rows_ref,
    weight_ref,
    att_ref,
    dq_ref,
    out_ref,
    rows_all,
    weight_all,
    kv_all,
    q_all,
    g_all,
    kv_t,
    score,
    prob,
    dscore,
    dquery,
    stats,
    rows_t,
    rows_tt,
    acc,
    keep,
    core_out,
    core_in,
    y_out,
    y_in,
    z_out,
    z_in,
    grad,
    send_sem,
    recv_sem,
):
    sec, seq, mp = place()
    copies = Copies(send_sem, recv_sem)
    yy = seq // 4
    core = lax.rem(seq, 2)
    across, other, along = seq_peers(sec, seq, mp)
    sec_peer = {d: (lax.rem(sec + d, 4), seq, mp) for d in (1, 2, 3)}
    mp_peer = {d: (sec, seq, lax.rem(mp + d, 4)) for d in (1, 2, 3)}
    own = sec * 4 + mp
    zhi = lax.rem(seq // 2, 2)
    turning = mp // 2 != zhi
    mirror = (seq // 4, own, lax.rem(seq, 4))
    aslant = {d: (sec, lax.rem(seq + 4 * d, 16) + 1 - 2 * core, mp) for d in (1, 2, 3)}

    barrier = pltpu.get_barrier_semaphore()
    peers = (
        [mp_peer[d] for d in (1, 2, 3)]
        + [sec_peer[d] for d in (1, 2, 3)]
        + [along[d] for d in (1, 2, 3)]
        + [aslant[d] for d in (1, 2, 3)]
        + [across, other]
    )
    for peer in peers:
        pl.semaphore_signal(barrier, inc=1, device_id=peer, device_id_type=MESH)

    @pl.when(turning)
    def _():
        pl.semaphore_signal(barrier, inc=1, device_id=mirror, device_id_type=MESH)

    rows_all[own] = rows_ref[...]
    weight_all[seq] = weight_ref[0]
    pl.semaphore_wait(barrier, len(peers) + turning.astype(jnp.int32))

    w_rows, kv_rows = weight_all.shape[1] // 2, kv_all.shape[1] // 2
    gather_w = [
        SeqGather(copies, weight_all, pl.ds(p * w_rows, w_rows), sec, seq, mp) for p in (0, 1)
    ]
    gather_kv = [
        SeqGather(copies, kv_all, pl.ds(p * kv_rows, kv_rows), sec, seq, mp) for p in (0, 1)
    ]
    sides = [(side, hops) for hops in (1, 2, 3) for side in (-1, 1)]
    line_slot = {key: copies.slot() for key in sides}
    along_x = {(key, d): copies.slot() for key in [(0, 0)] + sides for d in (1, 2, 3)}
    turn_slot = copies.slot()
    m_slot = {(j, d): copies.slot() for j in (0, 1) for d in (1, 2, 3)}
    x_slot = {(j, d): copies.slot() for j in (0, 1) for d in (1, 2, 3)}
    y_same = {d: copies.slot() for d in (1, 2, 3)}
    y_cross = {d: copies.slot() for d in (0, 1, 2, 3)}
    core_slot = [copies.slot() for _ in range(4)]
    y_slot = {d: copies.slot() for d in (1, 2, 3)}
    z_slot = [copies.slot() for _ in range(PIECES)]
    ag_slot = {(p, d): copies.slot() for p in range(PIECES) for d in (1, 2, 3)}
    cg_slot = {(p, d): copies.slot() for p in range(PIECES) for d in (0, 1, 2, 3)}

    tok = q_ref.shape[0]
    half = tok // SLOTS
    group = q_ref.shape[1] // HD
    lanes = group * half
    part_rows = 4 * tok
    scale = HD ** (-0.5)
    rate = scale * LOG2E

    def token_block(t):
        return rows_t.at[t // 2, pl.ds(pl.multiple_of(lax.rem(t, 2) * tok, 16), tok), :]

    def pass_on(e):
        block = token_block(sec * 4 + lax.rem(mp + 4 - e, 4))
        if e:
            copies.wait_recv(m_slot[e], block, mp_peer[e])
        for d in (1, 3, 2):
            copies.start(x_slot[e, d], block, block, sec_peer[d])

    def lane(i):
        return slice(i * lanes, (i + 1) * lanes)

    below = (sec, seq, jnp.maximum(mp - 1, 0))
    above = (sec, seq, jnp.minimum(mp + 1, 3))

    def there(key):
        side, hops = key
        return mp >= hops if side < 0 else mp + hops <= 3

    def rows_of(key):
        side, hops = key
        return rows_all.at[sec * 4 + mp + side * hops]

    def spread(key):
        for d in (1, 3, 2):
            copies.start_if(
                along_x[key, d],
                lambda: rows_of(key),
                sec_peer[d],
                lambda: there(key),
            )

    def from_line(hops):
        for side in (-1, 1):
            key = (side, hops)

            @pl.when(there(key))
            def _():
                copies.wait_recv(line_slot[key], rows_of(key), below if side < 0 else above)

            if hops < 3:
                to_line(key)
            spread(key)

    def to_line(key):
        side, hops = key
        copies.start_if(
            line_slot[side, hops + 1],
            lambda: rows_of(key),
            above if side < 0 else below,
            lambda: jnp.logical_and(there(key), mp < 3 if side < 0 else mp > 0),
        )

    to_line((-1, 0))
    to_line((1, 0))
    spread((0, 0))
    gather_w[0].begin_far()
    gather_w[0].begin_near()
    gather_w[1].begin_near()
    for i in range(SLOTS):
        for h in range(group):
            at = i * lanes + h * half
            rows = slice(i * half, (i + 1) * half)
            q_all[at : at + half, :] = q_ref[rows, h * HD : (h + 1) * HD]
            g_all[at : at + half, :] = g_ref[rows, h * HD : (h + 1) * HD]
    from_line(1)
    gather_w[1].begin_far()
    gather_w[0].relay_across()
    from_line(2)
    gather_w[0].relay_core(0)
    gather_w[1].relay_core(0)
    gather_w[1].relay_across()
    turn = copies.make(turn_slot, rows_all.at[own], token_block(seq), mirror)

    @pl.when(turning)
    def _():
        turn.start()

    from_line(3)
    gather_w[0].relay_core(1)
    gather_w[1].relay_core(1)

    first_far = 2 - 2 * zhi

    def far_block(j):
        return token_block(sec * 4 + first_far + j)

    def has_far(j):
        return jnp.logical_and(turning, lax.rem(mp, 2) == j)

    def begin_line():
        @pl.when(turning)
        def _():
            turn.wait_send()
            copies.wait_recv(turn_slot, token_block(own), mirror)

        for j in (0, 1):
            for d in (1, 3, 2):
                copies.start_if(
                    m_slot[j, d], lambda j=j: far_block(j), mp_peer[d], lambda j=j: has_far(j)
                )

    def pass_on(j):
        for d in (1, 2, 3):
            @pl.when(first_far + j == lax.rem(mp + 4 - d, 4))
            def _():
                copies.wait_recv(m_slot[j, d], far_block(j), mp_peer[d])

        for d in (1, 3, 2):
            copies.start(x_slot[j, d], far_block(j), far_block(j), sec_peer[d])

    begin_line()
    for key in [(0, 0)] + sides:

        @pl.when(there(key))
        def _():
            for d in (1, 3, 2):
                copies.wait_recv(along_x[key, d], rows_of(key), sec_peer[d])

    for p in (0, 1):
        for d in range(4):
            gather_w[p].end(d, 0)
            gather_w[p].end(d, 1)

    total = jnp.zeros((tok, 2 * HD), jnp.float32)
    for f in range(16):
        total += jnp.dot(rows_all[f], weight_all[f], preferred_element_type=jnp.float32)
    kv_all[seq] = total.astype(jnp.bfloat16)

    for p in (0, 1):
        gather_kv[p].begin_far()
    for p in (0, 1):
        gather_kv[p].begin_near()

    side_rows = 2 * tok

    def side_first(d, t):
        return lax.rem(yy + 4 - d, 4) * 4 + 2 * (zhi if t == 0 else 1 - zhi)

    def keys_of(d, t):
        return kv_all[pl.ds(side_first(d, t), 2)].reshape(side_rows, 2 * HD)

    skew = lax.broadcasted_iota(jnp.int32, (half, lanes), 0) - lax.rem(
        lax.broadcasted_iota(jnp.int32, (half, lanes), 1), half
    )
    peaks = [jnp.full((8, lanes), -1e30, jnp.float32) for _ in range(SLOTS)]

    def look(d, t):
        for p in (0, 1):
            gather_kv[p].end(d, t)
        side_kv = keys_of(d, t)
        start = d * part_rows + t * side_rows
        kv_t[d, :, t * side_rows : (t + 1) * side_rows] = side_kv.T
        first = side_first(d, t) * SLOTS
        for i in range(SLOTS):
            raw = contract(side_kv[:, :HD], q_all[lane(i), :], 1, 1)
            for b in range(side_rows // half):
                ahead = (order[seq * SLOTS + i] - order[first + b]) * half
                seen = jnp.where(skew <= ahead, raw[b * half : (b + 1) * half, :], -1e30)
                at = start + b * half
                score[at : at + half, lane(i)] = seen
                peaks[i] = jnp.maximum(
                    peaks[i], jnp.max(seen.reshape(half // 8, 8, lanes), axis=0)
                )

    def along_y():
        token_block(seq)[...] = rows_all[seq]
        for d in (1, 3, 2):
            aim = lax.rem(seq + 4 * d, 16)
            copies.start(y_same[d], rows_all.at[aim], token_block(seq), along[d])
            aim = aim + 1 - 2 * core
            copies.start(y_cross[d], rows_all.at[aim], token_block(seq), aslant[d])
        copies.start(y_cross[0], rows_all.at[seq + 1 - 2 * core], token_block(seq), other)

    def end_blocks():
        for d in (1, 3, 2):
            copies.wait_recv(y_same[d], token_block(seq), along[d])
            copies.wait_recv(y_cross[d], token_block(seq), aslant[d])
        copies.wait_recv(y_cross[0], token_block(seq), other)
        for j in (0, 1):
            for d in (1, 3, 2):
                copies.wait_recv(x_slot[j, d], far_block(j), sec_peer[d])

    gather_kv[0].relay_core(0)
    pass_on(0)
    pass_on(1)
    gather_kv[0].relay_across()
    gather_kv[1].relay_core(0)
    gather_kv[1].relay_across()

    look(0, 0)
    look(1, 0)
    gather_kv[0].relay_core(1)
    look(3, 0)
    gather_kv[1].relay_core(1)
    along_y()
    look(2, 0)
    for d in (0, 1, 3, 2):
        look(d, 1)
    for i in range(SLOTS):
        peak = jnp.max(peaks[i], axis=0, keepdims=True)
        total = jnp.zeros((8, lanes), jnp.float32)
        for d in range(4):
            at = slice(d * part_rows, (d + 1) * part_rows)
            expo = jnp.exp2((score[at, lane(i)] - peak) * rate)
            score[at, lane(i)] = expo
            total += jnp.sum(expo.reshape(part_rows // 8, 8, lanes), axis=0)
        part = 1.0 / jnp.sum(total, axis=0, keepdims=True)
        out = jnp.zeros((HD, lanes), jnp.float32)
        for d in range(4):
            at = slice(d * part_rows, (d + 1) * part_rows)
            weights = (score[at, lane(i)] * part).astype(jnp.bfloat16)
            prob[at, lane(i)] = weights
            out += jnp.dot(kv_t[d, HD:], weights, preferred_element_type=jnp.float32)
        out = out.astype(jnp.bfloat16).astype(jnp.float32)
        delta = jnp.sum(g_all[lane(i), :].astype(jnp.float32).T * out, axis=0, keepdims=True)
        stats[0, :, lane(i)] = jnp.broadcast_to(delta, (8, lanes))
        stats[1, :, lane(i)] = jnp.broadcast_to(part * scale, (8, lanes))
        out = out.T.astype(jnp.bfloat16)
        for h in range(group):
            att_ref[i * half : (i + 1) * half, h * HD : (h + 1) * HD] = out[
                h * half : (h + 1) * half, :
            ]

    def back(d, between=None):
        part = (4 - d) % 4
        rows = slice(part * part_rows, (part + 1) * part_rows)
        values = jnp.concatenate([keys_of(part, t)[:, HD:] for t in (0, 1)], axis=0)
        for i in range(SLOTS):
            dprob = contract(values, g_all[lane(i), :], 1, 1)
            dscore[:, lane(i)] = (
                score[rows, lane(i)]
                * stats[1, :1, lane(i)]
                * (dprob - stats[0, :1, lane(i)])
            ).astype(jnp.bfloat16)
        if between:
            send_along(between)
        dkey = jnp.dot(dscore[...], q_all[...], preferred_element_type=jnp.float32)
        dvalue = jnp.dot(prob[rows, :], g_all[...], preferred_element_type=jnp.float32)
        for t, side in ((0, zhi), (1, 1 - zhi)):
            rows_here = slice(t * side_rows, (t + 1) * side_rows)
            acc[side, :, :, :HD] = dkey[rows_here].reshape(2, tok, HD)
            acc[side, :, :, HD:] = dvalue[rows_here].reshape(2, tok, HD)
        core_out[d] = acc[:, 1 - core].astype(jnp.bfloat16)
        copies.start(core_slot[d], core_out.at[d], core_in.at[d], other)
        keep[d] = acc[:, core]
        more = jnp.dot(kv_t[part, :HD], dscore[...], preferred_element_type=jnp.float32)
        if d == 2:
            dquery[...] = more
        else:
            dquery[...] += more

    def send_along(d):
        copies.wait_recv(core_slot[d], core_in.at[d], other)
        y_out[d - 1] = (keep[d] + core_in[d].astype(jnp.float32)).astype(jnp.bfloat16)
        copies.start(y_slot[d], y_out.at[d - 1], y_in.at[d - 1], along[d])

    back(2)
    back(1, between=2)
    back(3, between=1)
    back(0, between=3)
    for i in range(SLOTS):
        turned = dquery[:, lane(i)].T.astype(jnp.bfloat16)
        for h in range(group):
            dq_ref[i * half : (i + 1) * half, h * HD : (h + 1) * HD] = turned[
                h * half : (h + 1) * half, :
            ]
    copies.wait_recv(core_slot[0], core_in.at[0], other)
    for d in (1, 3, 2):
        copies.wait_recv(y_slot[d], y_in.at[d - 1], along[d])

    piece = tok // PIECES

    def piece_rows(p):
        return slice(p * piece, (p + 1) * piece)

    for p in range(PIECES):
        rows = piece_rows(p)
        total = keep[0, :, rows] + core_in[0, :, rows].astype(jnp.float32)
        for d in (1, 2, 3):
            total += y_in[d - 1, :, rows].astype(jnp.float32)
        z_out[p] = total.astype(jnp.bfloat16)
        copies.start(z_slot[p], z_out.at[p], z_in.at[p], across)
    end_blocks()
    for k in range(8):
        rows_tt[k] = rows_t[k].T
    for p in range(PIECES):
        copies.wait_recv(z_slot[p], z_in.at[p], across)
        grad[yy, :, core, piece_rows(p)] = (
            z_out[p].astype(jnp.float32) + z_in[p].astype(jnp.float32)
        ).astype(jnp.bfloat16)
        mine = grad.at[yy, :, core, piece_rows(p)]
        for d in (1, 3, 2):
            copies.start(ag_slot[p, d], mine, mine, along[d])
        copies.start(cg_slot[p, 0], mine, mine, other)
    for p in range(PIECES):
        for d in (1, 3, 2):
            block = grad.at[lax.rem(yy + 4 - d, 4), :, core, piece_rows(p)]
            copies.wait_recv(ag_slot[p, d], block, along[d])
            copies.start(cg_slot[p, d], block, block, other)
    for d in (0, 1, 3, 2):
        for p in range(PIECES):
            copies.wait_recv(cg_slot[p, d], grad.at[0, :, 0, piece_rows(p)], other)
        yt = lax.rem(yy + 4 - d, 4)
        more = sum(
            jnp.dot(
                rows_tt[2 * yt + t],
                grad[yt, t].reshape(2 * tok, 2 * HD),
                preferred_element_type=jnp.float32,
            )
            for t in (0, 1)
        )
        if d == 0:
            out_ref[...] = more
        else:
            out_ref[...] += more

    copies.finish()


def layer(order, queries, out_grad, rows, weight):
    tok, cols = queries.shape
    feat = rows.shape[1]
    keys = 16 * tok
    lanes = cols // HD * tok
    sems = 4 * 15 + 6 + 21 + 1 + 19 + 4 + 3 + PIECES * 8
    vmem = pl.BlockSpec(memory_space=pltpu.VMEM)
    half = (2, tok, 2 * HD)
    pieces = (PIECES, 2, tok // PIECES, 2 * HD)
    return pl.pallas_call(
        layer_kernel,
        out_shape=(
            jax.ShapeDtypeStruct((tok, cols), jnp.bfloat16),
            jax.ShapeDtypeStruct((tok, cols), jnp.bfloat16),
            jax.ShapeDtypeStruct((feat, 2 * HD), jnp.float32),
        ),
        in_specs=[pl.BlockSpec(memory_space=pltpu.SMEM)] + [vmem] * 4,
        out_specs=(vmem, vmem, vmem),
        scratch_shapes=[
            pltpu.VMEM((16, tok, feat), jnp.bfloat16),
            pltpu.VMEM((16, feat, 2 * HD), jnp.bfloat16),
            pltpu.VMEM((16, tok, 2 * HD), jnp.bfloat16),
            pltpu.VMEM((lanes, HD), jnp.bfloat16),
            pltpu.VMEM((lanes, HD), jnp.bfloat16),
            pltpu.VMEM((4, 2 * HD, keys // 4), jnp.bfloat16),
            pltpu.VMEM((keys, lanes), jnp.float32),
            pltpu.VMEM((keys, lanes), jnp.bfloat16),
            pltpu.VMEM((keys // 4, lanes), jnp.bfloat16),
            pltpu.VMEM((HD, lanes), jnp.float32),
            pltpu.VMEM((2, 8, lanes), jnp.float32),
            pltpu.VMEM((8, 2 * tok, feat), jnp.bfloat16),
            pltpu.VMEM((8, feat, 2 * tok), jnp.bfloat16),
            pltpu.VMEM((2,) + half, jnp.float32),
            pltpu.VMEM((4,) + half, jnp.float32),
            pltpu.VMEM((4,) + half, jnp.bfloat16),
            pltpu.VMEM((4,) + half, jnp.bfloat16),
            pltpu.VMEM((3,) + half, jnp.bfloat16),
            pltpu.VMEM((3,) + half, jnp.bfloat16),
            pltpu.VMEM(pieces, jnp.bfloat16),
            pltpu.VMEM(pieces, jnp.bfloat16),
            pltpu.VMEM((4, 2) + half, jnp.bfloat16),
            pltpu.SemaphoreType.DMA((sems,)),
            pltpu.SemaphoreType.DMA((sems,)),
        ],
        compiler_params=pltpu.CompilerParams(
            collective_id=0, has_side_effects=True, vmem_limit_bytes=VMEM_LIMIT
        ),
        name="layer",
    )(order, queries, out_grad, rows, weight)


def body(rows40, queries, kv_weight, out_grad, block_order):
    attended, query_grad, grad = layer(block_order, queries[0], out_grad[0], rows40, kv_weight)
    return (attended[None], query_grad[None], grad[None])


def solution(mesh):
    return jax.shard_map(
        body,
        mesh=mesh,
        in_specs=(
            P("seq", ("section", "mp")),
            P("section", "seq", "mp"),
            P("section", "seq", "mp"),
            P("section", "seq", "mp"),
            P(),
        ),
        out_specs=(P("section", "seq", "mp"), P("section", "seq", "mp"), P("section", "seq", "mp")),
        check_vma=False,
    )
```

```python
import functools

import jax
import jax.numpy as jnp
from jax import lax
import jax.experimental.pallas as pl
import jax.experimental.pallas.tpu as pltpu
from jax.sharding import PartitionSpec as P

HD = 128
SLOTS = 4
PIECES = 4
VMEM_LIMIT = 60 * 2**20
MESH = pl.DeviceIdType.MESH
LOG2E = 1.4426950408889634


def contract(left, right, left_dim, right_dim):
    return lax.dot_general(
        left,
        right,
        (((left_dim,), (right_dim,)), ((), ())),
        preferred_element_type=jnp.float32,
    )


class Copies:
    def __init__(self, send_sem, recv_sem):
        self.send_sem = send_sem
        self.recv_sem = recv_sem
        self.count = 0
        self.started = []
        self.guarded = []

    def slot(self):
        self.count += 1
        return self.count - 1

    def make(self, slot, src, dst, device):
        return pltpu.make_async_remote_copy(
            src_ref=src,
            dst_ref=dst,
            send_sem=self.send_sem.at[slot],
            recv_sem=self.recv_sem.at[slot],
            device_id=device,
            device_id_type=MESH,
        )

    def start(self, slot, src, dst, device):
        copy = self.make(slot, src, dst, device)
        copy.start()
        self.started.append(copy)

    def wait_recv(self, slot, buf, device):
        self.make(slot, buf, buf, device).wait_recv()

    def start_if(self, slot, ref, device, condition):
        @pl.when(condition())
        def _():
            self.make(slot, ref(), ref(), device).start()

        self.guarded.append((slot, ref, device, condition))

    def finish(self):
        for copy in self.started:
            copy.wait_send()
        for slot, ref, device, condition in self.guarded:

            @pl.when(condition())
            def _():
                self.make(slot, ref(), ref(), device).wait_send()


def place():
    sec = lax.axis_index("section")
    seq = lax.axis_index("seq")
    mp = lax.axis_index("mp")
    return sec, seq, mp


def greet(peers):
    barrier = pltpu.get_barrier_semaphore()
    for peer in peers:
        pl.semaphore_signal(barrier, inc=1, device_id=peer, device_id_type=MESH)
    pl.semaphore_wait(barrier, len(peers))


def seq_peers(sec, seq, mp):
    zhi = lax.rem(seq // 2, 2)
    core = lax.rem(seq, 2)
    across = (sec, seq + 2 - 4 * zhi, mp)
    other = (sec, seq + 1 - 2 * core, mp)
    along = {d: (sec, lax.rem(seq + 4 * d, 16), mp) for d in (1, 2, 3)}
    return across, other, along


class SeqGather:
    def __init__(self, copies, buf, rows, sec, seq, mp):
        self.copies = copies
        self.buf = buf
        self.rows = rows
        self.seq = seq
        self.across, self.other, self.along = seq_peers(sec, seq, mp)
        self.z_slot = copies.slot()
        self.y_slot = {(t, d): copies.slot() for t in (0, 1) for d in (1, 2, 3)}
        self.c_slot = {(t, d): copies.slot() for t in (0, 1) for d in (0, 1, 2, 3)}

    def block(self, t, d):
        owner = lax.rem(self.seq + 16 - 4 * d, 16)
        if t:
            owner = owner + 2 - 4 * lax.rem(owner // 2, 2)
        return self.buf.at[owner, self.rows]

    def send(self, slot, t, d, device):
        block = self.block(t, d)
        self.copies.start(slot, block, block, device)

    def begin_far(self):
        self.send(self.z_slot, 0, 0, self.across)

    def begin_near(self, t=0):
        for d in (1, 3, 2):
            self.send(self.y_slot[t, d], t, 0, self.along[d])
        self.send(self.c_slot[t, 0], t, 0, self.other)

    def relay_across(self):
        self.copies.wait_recv(self.z_slot, self.block(1, 0), self.across)
        self.begin_near(1)

    def relay_core(self, t):
        for d in (1, 3, 2):
            self.copies.wait_recv(self.y_slot[t, d], self.block(t, d), self.along[d])
            self.send(self.c_slot[t, d], t, d, self.other)

    def end(self, d, t):
        self.copies.wait_recv(self.c_slot[t, d], self.block(t, d), self.other)


def layer_kernel(
    order,
    q_ref,
    g_ref,
    rows_ref,
    weight_ref,
    att_ref,
    dq_ref,
    out_ref,
    rows_all,
    weight_all,
    kv_all,
    q_all,
    g_all,
    kv_t,
    score,
    prob,
    dscore,
    dquery,
    stats,
    rows_t,
    rows_tt,
    acc,
    keep,
    core_out,
    core_in,
    y_out,
    y_in,
    z_out,
    z_in,
    grad,
    send_sem,
    recv_sem,
):
    sec, seq, mp = place()
    copies = Copies(send_sem, recv_sem)
    yy = seq // 4
    core = lax.rem(seq, 2)
    across, other, along = seq_peers(sec, seq, mp)
    sec_peer = {d: (lax.rem(sec + d, 4), seq, mp) for d in (1, 2, 3)}
    mp_peer = {d: (sec, seq, lax.rem(mp + d, 4)) for d in (1, 2, 3)}
    own = sec * 4 + mp
    zhi = lax.rem(seq // 2, 2)
    turning = mp // 2 != zhi
    mirror = (seq // 4, own, lax.rem(seq, 4))
    aslant = {d: (sec, lax.rem(seq + 4 * d, 16) + 1 - 2 * core, mp) for d in (1, 2, 3)}

    barrier = pltpu.get_barrier_semaphore()
    peers = (
        [mp_peer[d] for d in (1, 2, 3)]
        + [sec_peer[d] for d in (1, 2, 3)]
        + [along[d] for d in (1, 2, 3)]
        + [aslant[d] for d in (1, 2, 3)]
        + [across, other]
    )
    for peer in peers:
        pl.semaphore_signal(barrier, inc=1, device_id=peer, device_id_type=MESH)

    @pl.when(turning)
    def _():
        pl.semaphore_signal(barrier, inc=1, device_id=mirror, device_id_type=MESH)

    rows_all[own] = rows_ref[...]
    weight_all[seq] = weight_ref[0]
    pl.semaphore_wait(barrier, len(peers) + turning.astype(jnp.int32))

    w_rows, kv_rows = weight_all.shape[1] // 2, kv_all.shape[1] // 2
    gather_w = [
        SeqGather(copies, weight_all, pl.ds(p * w_rows, w_rows), sec, seq, mp) for p in (0, 1)
    ]
    gather_kv = [
        SeqGather(copies, kv_all, pl.ds(p * kv_rows, kv_rows), sec, seq, mp) for p in (0, 1)
    ]
    sides = [(side, hops) for hops in (1, 2, 3) for side in (-1, 1)]
    line_slot = {key: copies.slot() for key in sides}
    along_x = {(key, d): copies.slot() for key in [(0, 0)] + sides for d in (1, 2, 3)}
    turn_slot = copies.slot()
    m_slot = {(j, d): copies.slot() for j in (0, 1) for d in (1, 2, 3)}
    x_slot = {(j, d): copies.slot() for j in (0, 1) for d in (1, 2, 3)}
    y_same = {d: copies.slot() for d in (1, 2, 3)}
    y_cross = {d: copies.slot() for d in (0, 1, 2, 3)}
    core_slot = [copies.slot() for _ in range(4)]
    y_slot = {d: copies.slot() for d in (1, 2, 3)}
    z_slot = [copies.slot() for _ in range(PIECES)]
    ag_slot = {(p, d): copies.slot() for p in range(PIECES) for d in (1, 2, 3)}
    cg_slot = {(p, d): copies.slot() for p in range(PIECES) for d in (0, 1, 2, 3)}

    tok = q_ref.shape[0]
    half = tok // SLOTS
    group = q_ref.shape[1] // HD
    lanes = group * half
    part_rows = 4 * tok
    scale = HD ** (-0.5)
    rate = scale * LOG2E

    def token_block(t):
        return rows_t.at[t // 2, pl.ds(pl.multiple_of(lax.rem(t, 2) * tok, 16), tok), :]

    def pass_on(e):
        block = token_block(sec * 4 + lax.rem(mp + 4 - e, 4))
        if e:
            copies.wait_recv(m_slot[e], block, mp_peer[e])
        for d in (1, 3, 2):
            copies.start(x_slot[e, d], block, block, sec_peer[d])

    def lane(i):
        return slice(i * lanes, (i + 1) * lanes)

    below = (sec, seq, jnp.maximum(mp - 1, 0))
    above = (sec, seq, jnp.minimum(mp + 1, 3))

    def there(key):
        side, hops = key
        return mp >= hops if side < 0 else mp + hops <= 3

    def rows_of(key):
        side, hops = key
        return rows_all.at[sec * 4 + mp + side * hops]

    def spread(key):
        for d in (1, 3, 2):
            copies.start_if(
                along_x[key, d],
                lambda: rows_of(key),
                sec_peer[d],
                lambda: there(key),
            )

    def from_line(hops):
        for side in (-1, 1):
            key = (side, hops)

            @pl.when(there(key))
            def _():
                copies.wait_recv(line_slot[key], rows_of(key), below if side < 0 else above)

            if hops < 3:
                to_line(key)
            spread(key)

    def to_line(key):
        side, hops = key
        copies.start_if(
            line_slot[side, hops + 1],
            lambda: rows_of(key),
            above if side < 0 else below,
            lambda: jnp.logical_and(there(key), mp < 3 if side < 0 else mp > 0),
        )

    to_line((-1, 0))
    to_line((1, 0))
    spread((0, 0))
    gather_w[0].begin_far()
    gather_w[0].begin_near()
    gather_w[1].begin_near()
    for i in range(SLOTS):
        for h in range(group):
            at = i * lanes + h * half
            rows = slice(i * half, (i + 1) * half)
            q_all[at : at + half, :] = q_ref[rows, h * HD : (h + 1) * HD]
            g_all[at : at + half, :] = g_ref[rows, h * HD : (h + 1) * HD]
    from_line(1)
    gather_w[1].begin_far()
    gather_w[0].relay_across()
    from_line(2)
    gather_w[0].relay_core(0)
    gather_w[1].relay_core(0)
    gather_w[1].relay_across()
    turn = copies.make(turn_slot, rows_all.at[own], token_block(seq), mirror)

    @pl.when(turning)
    def _():
        turn.start()

    from_line(3)
    gather_w[0].relay_core(1)
    gather_w[1].relay_core(1)

    first_far = 2 - 2 * zhi

    def far_block(j):
        return token_block(sec * 4 + first_far + j)

    def has_far(j):
        return jnp.logical_and(turning, lax.rem(mp, 2) == j)

    def begin_line():
        @pl.when(turning)
        def _():
            turn.wait_send()
            copies.wait_recv(turn_slot, token_block(own), mirror)

        for j in (0, 1):
            for d in (1, 3, 2):
                copies.start_if(
                    m_slot[j, d], lambda j=j: far_block(j), mp_peer[d], lambda j=j: has_far(j)
                )

    def pass_on(j):
        for d in (1, 2, 3):
            @pl.when(first_far + j == lax.rem(mp + 4 - d, 4))
            def _():
                copies.wait_recv(m_slot[j, d], far_block(j), mp_peer[d])

        for d in (1, 3, 2):
            copies.start(x_slot[j, d], far_block(j), far_block(j), sec_peer[d])

    begin_line()
    for p in (0, 1):
        for d in range(4):
            gather_w[p].end(d, 0)
            gather_w[p].end(d, 1)

    keep[0, 0] = jnp.zeros((tok, 2 * HD), jnp.float32)
    for key in [(0, 0)] + sides:

        @pl.when(there(key))
        def _():
            for d in (1, 3, 2):
                copies.wait_recv(along_x[key, d], rows_of(key), sec_peer[d])
            more = jnp.zeros((tok, 2 * HD), jnp.float32)
            for d in range(4):
                f = lax.rem(sec + d, 4) * 4 + mp + key[0] * key[1]
                more += jnp.dot(rows_all[f], weight_all[f], preferred_element_type=jnp.float32)
            keep[0, 0] += more

    total = keep[0, 0]
    kv_all[seq] = total.astype(jnp.bfloat16)

    for p in (0, 1):
        gather_kv[p].begin_far()
    for p in (0, 1):
        gather_kv[p].begin_near()

    side_rows = 2 * tok

    def side_first(d, t):
        return lax.rem(yy + 4 - d, 4) * 4 + 2 * (zhi if t == 0 else 1 - zhi)

    def keys_of(d, t):
        return kv_all[pl.ds(side_first(d, t), 2)].reshape(side_rows, 2 * HD)

    skew = lax.broadcasted_iota(jnp.int32, (half, lanes), 0) - lax.rem(
        lax.broadcasted_iota(jnp.int32, (half, lanes), 1), half
    )
    peaks = [jnp.full((8, lanes), -1e30, jnp.float32) for _ in range(SLOTS)]

    def look(d, t):
        for p in (0, 1):
            gather_kv[p].end(d, t)
        side_kv = keys_of(d, t)
        start = d * part_rows + t * side_rows
        kv_t[d, :, t * side_rows : (t + 1) * side_rows] = side_kv.T
        first = side_first(d, t) * SLOTS
        for i in range(SLOTS):
            raw = contract(side_kv[:, :HD], q_all[lane(i), :], 1, 1)
            for b in range(side_rows // half):
                ahead = (order[seq * SLOTS + i] - order[first + b]) * half
                seen = jnp.where(skew <= ahead, raw[b * half : (b + 1) * half, :], -1e30)
                at = start + b * half
                score[at : at + half, lane(i)] = seen
                peaks[i] = jnp.maximum(
                    peaks[i], jnp.max(seen.reshape(half // 8, 8, lanes), axis=0)
                )

    def along_y():
        token_block(seq)[...] = rows_all[seq]
        for d in (1, 3, 2):
            aim = lax.rem(seq + 4 * d, 16)
            copies.start(y_same[d], rows_all.at[aim], token_block(seq), along[d])
            aim = aim + 1 - 2 * core
            copies.start(y_cross[d], rows_all.at[aim], token_block(seq), aslant[d])
        copies.start(y_cross[0], rows_all.at[seq + 1 - 2 * core], token_block(seq), other)

    def end_blocks():
        for d in (1, 3, 2):
            copies.wait_recv(y_same[d], token_block(seq), along[d])
            copies.wait_recv(y_cross[d], token_block(seq), aslant[d])
        copies.wait_recv(y_cross[0], token_block(seq), other)
        for j in (0, 1):
            for d in (1, 3, 2):
                copies.wait_recv(x_slot[j, d], far_block(j), sec_peer[d])

    gather_kv[0].relay_core(0)
    pass_on(0)
    pass_on(1)
    gather_kv[0].relay_across()
    gather_kv[1].relay_core(0)
    gather_kv[1].relay_across()

    look(0, 0)
    look(1, 0)
    gather_kv[0].relay_core(1)
    look(3, 0)
    gather_kv[1].relay_core(1)
    along_y()
    look(2, 0)
    for d in (0, 1, 3, 2):
        look(d, 1)
    for i in range(SLOTS):
        peak = jnp.max(peaks[i], axis=0, keepdims=True)
        total = jnp.zeros((8, lanes), jnp.float32)
        for d in range(4):
            at = slice(d * part_rows, (d + 1) * part_rows)
            expo = jnp.exp2((score[at, lane(i)] - peak) * rate)
            score[at, lane(i)] = expo
            total += jnp.sum(expo.reshape(part_rows // 8, 8, lanes), axis=0)
        part = 1.0 / jnp.sum(total, axis=0, keepdims=True)
        out = jnp.zeros((HD, lanes), jnp.float32)
        for d in range(4):
            at = slice(d * part_rows, (d + 1) * part_rows)
            weights = (score[at, lane(i)] * part).astype(jnp.bfloat16)
            prob[at, lane(i)] = weights
            out += jnp.dot(kv_t[d, HD:], weights, preferred_element_type=jnp.float32)
        out = out.astype(jnp.bfloat16).astype(jnp.float32)
        delta = jnp.sum(g_all[lane(i), :].astype(jnp.float32).T * out, axis=0, keepdims=True)
        stats[0, :, lane(i)] = jnp.broadcast_to(delta, (8, lanes))
        stats[1, :, lane(i)] = jnp.broadcast_to(part * scale, (8, lanes))
        out = out.T.astype(jnp.bfloat16)
        for h in range(group):
            att_ref[i * half : (i + 1) * half, h * HD : (h + 1) * HD] = out[
                h * half : (h + 1) * half, :
            ]

    def back(d, between=None):
        part = (4 - d) % 4
        rows = slice(part * part_rows, (part + 1) * part_rows)
        values = jnp.concatenate([keys_of(part, t)[:, HD:] for t in (0, 1)], axis=0)
        for i in range(SLOTS):
            dprob = contract(values, g_all[lane(i), :], 1, 1)
            dscore[:, lane(i)] = (
                score[rows, lane(i)]
                * stats[1, :1, lane(i)]
                * (dprob - stats[0, :1, lane(i)])
            ).astype(jnp.bfloat16)
        if between:
            send_along(between)
        dkey = jnp.dot(dscore[...], q_all[...], preferred_element_type=jnp.float32)
        dvalue = jnp.dot(prob[rows, :], g_all[...], preferred_element_type=jnp.float32)
        for t, side in ((0, zhi), (1, 1 - zhi)):
            rows_here = slice(t * side_rows, (t + 1) * side_rows)
            acc[side, :, :, :HD] = dkey[rows_here].reshape(2, tok, HD)
            acc[side, :, :, HD:] = dvalue[rows_here].reshape(2, tok, HD)
        core_out[d] = acc[:, 1 - core].astype(jnp.bfloat16)
        copies.start(core_slot[d], core_out.at[d], core_in.at[d], other)
        keep[d] = acc[:, core]
        more = jnp.dot(kv_t[part, :HD], dscore[...], preferred_element_type=jnp.float32)
        if d == 2:
            dquery[...] = more
        else:
            dquery[...] += more

    def send_along(d):
        copies.wait_recv(core_slot[d], core_in.at[d], other)
        y_out[d - 1] = (keep[d] + core_in[d].astype(jnp.float32)).astype(jnp.bfloat16)
        copies.start(y_slot[d], y_out.at[d - 1], y_in.at[d - 1], along[d])

    back(2)
    back(1, between=2)
    back(3, between=1)
    back(0, between=3)
    for i in range(SLOTS):
        turned = dquery[:, lane(i)].T.astype(jnp.bfloat16)
        for h in range(group):
            dq_ref[i * half : (i + 1) * half, h * HD : (h + 1) * HD] = turned[
                h * half : (h + 1) * half, :
            ]
    copies.wait_recv(core_slot[0], core_in.at[0], other)
    for d in (1, 3, 2):
        copies.wait_recv(y_slot[d], y_in.at[d - 1], along[d])

    piece = tok // PIECES

    def piece_rows(p):
        return slice(p * piece, (p + 1) * piece)

    for p in range(PIECES):
        rows = piece_rows(p)
        total = keep[0, :, rows] + core_in[0, :, rows].astype(jnp.float32)
        for d in (1, 2, 3):
            total += y_in[d - 1, :, rows].astype(jnp.float32)
        z_out[p] = total.astype(jnp.bfloat16)
        copies.start(z_slot[p], z_out.at[p], z_in.at[p], across)
    end_blocks()
    for k in range(8):
        rows_tt[k] = rows_t[k].T
    for p in range(PIECES):
        copies.wait_recv(z_slot[p], z_in.at[p], across)
        grad[yy, :, core, piece_rows(p)] = (
            z_out[p].astype(jnp.float32) + z_in[p].astype(jnp.float32)
        ).astype(jnp.bfloat16)
        mine = grad.at[yy, :, core, piece_rows(p)]
        for d in (1, 3, 2):
            copies.start(ag_slot[p, d], mine, mine, along[d])
        copies.start(cg_slot[p, 0], mine, mine, other)
    for p in range(PIECES):
        for d in (1, 3, 2):
            block = grad.at[lax.rem(yy + 4 - d, 4), :, core, piece_rows(p)]
            copies.wait_recv(ag_slot[p, d], block, along[d])
            copies.start(cg_slot[p, d], block, block, other)
    for d in (0, 1, 3, 2):
        for p in range(PIECES):
            copies.wait_recv(cg_slot[p, d], grad.at[0, :, 0, piece_rows(p)], other)
        yt = lax.rem(yy + 4 - d, 4)
        more = sum(
            jnp.dot(
                rows_tt[2 * yt + t],
                grad[yt, t].reshape(2 * tok, 2 * HD),
                preferred_element_type=jnp.float32,
            )
            for t in (0, 1)
        )
        if d == 0:
            out_ref[...] = more
        else:
            out_ref[...] += more

    copies.finish()


def layer(order, queries, out_grad, rows, weight):
    tok, cols = queries.shape
    feat = rows.shape[1]
    keys = 16 * tok
    lanes = cols // HD * tok
    sems = 4 * 15 + 6 + 21 + 1 + 19 + 4 + 3 + PIECES * 8
    vmem = pl.BlockSpec(memory_space=pltpu.VMEM)
    half = (2, tok, 2 * HD)
    pieces = (PIECES, 2, tok // PIECES, 2 * HD)
    return pl.pallas_call(
        layer_kernel,
        out_shape=(
            jax.ShapeDtypeStruct((tok, cols), jnp.bfloat16),
            jax.ShapeDtypeStruct((tok, cols), jnp.bfloat16),
            jax.ShapeDtypeStruct((feat, 2 * HD), jnp.float32),
        ),
        in_specs=[pl.BlockSpec(memory_space=pltpu.SMEM)] + [vmem] * 4,
        out_specs=(vmem, vmem, vmem),
        scratch_shapes=[
            pltpu.VMEM((16, tok, feat), jnp.bfloat16),
            pltpu.VMEM((16, feat, 2 * HD), jnp.bfloat16),
            pltpu.VMEM((16, tok, 2 * HD), jnp.bfloat16),
            pltpu.VMEM((lanes, HD), jnp.bfloat16),
            pltpu.VMEM((lanes, HD), jnp.bfloat16),
            pltpu.VMEM((4, 2 * HD, keys // 4), jnp.bfloat16),
            pltpu.VMEM((keys, lanes), jnp.float32),
            pltpu.VMEM((keys, lanes), jnp.bfloat16),
            pltpu.VMEM((keys // 4, lanes), jnp.bfloat16),
            pltpu.VMEM((HD, lanes), jnp.float32),
            pltpu.VMEM((2, 8, lanes), jnp.float32),
            pltpu.VMEM((8, 2 * tok, feat), jnp.bfloat16),
            pltpu.VMEM((8, feat, 2 * tok), jnp.bfloat16),
            pltpu.VMEM((2,) + half, jnp.float32),
            pltpu.VMEM((4,) + half, jnp.float32),
            pltpu.VMEM((4,) + half, jnp.bfloat16),
            pltpu.VMEM((4,) + half, jnp.bfloat16),
            pltpu.VMEM((3,) + half, jnp.bfloat16),
            pltpu.VMEM((3,) + half, jnp.bfloat16),
            pltpu.VMEM(pieces, jnp.bfloat16),
            pltpu.VMEM(pieces, jnp.bfloat16),
            pltpu.VMEM((4, 2) + half, jnp.bfloat16),
            pltpu.SemaphoreType.DMA((sems,)),
            pltpu.SemaphoreType.DMA((sems,)),
        ],
        compiler_params=pltpu.CompilerParams(
            collective_id=0, has_side_effects=True, vmem_limit_bytes=VMEM_LIMIT
        ),
        name="layer",
    )(order, queries, out_grad, rows, weight)


def body(rows40, queries, kv_weight, out_grad, block_order):
    attended, query_grad, grad = layer(block_order, queries[0], out_grad[0], rows40, kv_weight)
    return (attended[None], query_grad[None], grad[None])


def solution(mesh):
    return jax.shard_map(
        body,
        mesh=mesh,
        in_specs=(
            P("seq", ("section", "mp")),
            P("section", "seq", "mp"),
            P("section", "seq", "mp"),
            P("section", "seq", "mp"),
            P(),
        ),
        out_specs=(P("section", "seq", "mp"), P("section", "seq", "mp"), P("section", "seq", "mp")),
        check_vma=False,
    )
```
